512 devices in a mesh: dp: 8 (over x_hi, y), ctx: 64 (over x_lo, z, core).
Axes of the slice: x: 4 (x_hi: 2, x_lo: 2; x = x_hi * 2 + x_lo), y: 4, z: 16, core: 2. Of those that a mesh axis runs over, the one named last changes fastest.
Arguments:
- queries: bfloat16 [8, 8192, 2048], P('dp', 'ctx'), may hold values from -6 to 6
- key_vectors: bfloat16 [8, 8192, 256], P('dp', 'ctx'), may hold values from -6 to 6
- value_vectors: bfloat16 [8, 8192, 256], P('dp', 'ctx'), may hold values from -6 to 6
- out_grad: bfloat16 [8, 8192, 2048], P('dp', 'ctx'), may hold values from -6 to 6
- sink_logits: float32 [32], replicated, may hold values from 2 to 7
- lengths: int32 [8, 16], replicated, may hold values from 1 to 512, 5120 in all within a row
- route_plan: int32 [16], replicated, may hold values from 0 to 7
Outputs:
- attn_out: bfloat16 [8, 8192, 2048], P('dp', 'ctx')
- query_grad: bfloat16 [8, 8192, 2048], P('dp', 'ctx')
- key_grad: bfloat16 [8, 8192, 256], P('dp', 'ctx')
- value_grad: bfloat16 [8, 8192, 256], P('dp', 'ctx')
- sink_grad: float32 [32], replicated
The draws below stay inside these ranges and needn't reach their ends.
Inputs may be any that keep to these rules, and one draw needn't show every extreme that they name: The 16 lengths of each generating group sum to 5120, and the largest is 512.
All inputs are finite; a program needn't handle non-finite values.
Results may differ from the reference program's by a relative error of at most 0.035.
Values may be sent and summed in bfloat16 or wider, within the bound.
No kernel may reach another device: no remote copies, remote signals or barrier semaphores. Data moves between devices by JAX's collectives and lax.ppermute only.
A program may use at most 64 MiB of HBM per device.

```python
import math
from functools import partial
import jax
import jax.numpy as jnp
import numpy as np
from jax import lax

D_HEAD = 64
Q_HEADS = 32
KV_HEADS = 4
HEAD_GROUP = 8
SLOTS = 16
CAP = 512
GTOK = 8192
N_DP = 8


def draw_queries(key, part):
    key = jax.random.fold_in(key, 11)
    full_shape = (N_DP, GTOK, Q_HEADS * D_HEAD)
    return jnp.clip(jax.random.normal(key, full_shape, jnp.float32), -5.0, 5.0).astype(jnp.bfloat16)


def draw_key_vectors(key, part):
    key = jax.random.fold_in(key, 23)
    full_shape = (N_DP, GTOK, KV_HEADS * D_HEAD)
    return jnp.clip(jax.random.normal(key, full_shape, jnp.float32), -5.0, 5.0).astype(jnp.bfloat16)


def place_ends(entries, key, low, high):
    shape = entries.shape
    spot = [jax.random.randint(jax.random.fold_in(key, axis), (), 0, shape[axis]) for axis in range(len(shape))]
    entries = entries.at[tuple(spot)].set(low)
    longest = shape.index(max(shape))
    spot[longest] = (spot[longest] + 1) % shape[longest]
    return entries.at[tuple(spot)].set(high)


def levels(key, extent, split, low, largest):
    def one(axis_at, parts):
        heights = jax.random.uniform(jax.random.fold_in(jax.random.fold_in(key, 6), axis_at), (parts,), jnp.float32, low / len(split), largest / len(split))
        return jnp.repeat(jnp.exp(heights), extent[axis_at] // parts).reshape((-1,) + (1,) * (len(extent) - axis_at - 1))

    level = one(*split[0])
    for cut in split[1:]:
        level = level * one(*cut)
    return level


def profile(amount, total, reach, lean):
    loads = [(1 << 20) // math.isqrt(grade ** lean) + 1 for grade in range(2, amount + 1)]
    rest, holding = total - reach - (amount - 1), [1] * (amount - 1)
    while rest > 0:
        free = [i for i in range(amount - 1) if holding[i] < reach]
        mass, left = sum([loads[i] for i in free]), rest
        for i in free:
            addition = min(reach - holding[i], max(1, left * loads[i] // mass), rest)
            holding[i] = holding[i] + addition
            rest = rest - addition
    return np.array([reach] + holding)


def ragged(key, count, total, bound, skew):
    if count == 2:
        one = jax.random.randint(key, (), max(1, total - bound), min(bound, total - 1) + 1)
        return jnp.stack([one, total - one])
    sizes = jnp.asarray(profile(count, total, bound, skew), jnp.int32)
    pairs = (count - 1) // 2
    source_of, taker = sizes[1:1 + 2 * pairs:2], sizes[2:2 + 2 * pairs:2]
    margin = jnp.minimum(source_of - 1, bound - taker)
    shifted = jax.random.randint(jax.random.fold_in(key, 1), (pairs,), 0, 1 << 20) % (margin + 1)
    sizes = sizes.at[1:1 + 2 * pairs:2].set(source_of - shifted).at[2:2 + 2 * pairs:2].set(taker + shifted)
    return sizes[jax.random.permutation(jax.random.fold_in(key, 2), count)]


def centred(stream_key, dims, width, bound, shards=(), held_as=jnp.bfloat16):
    values = jax.random.normal(stream_key, dims, jnp.float32) * width
    if len(shards) > 0:
        values = levels(stream_key, dims, shards, -0.22, 0.18) * values
    return jnp.clip(values, min=-bound, max=bound).astype(held_as)


def setup_inputs(seed: int = 0) -> dict:
    key_of = jax.random.split(jax.random.key(seed), 8)
    queries = draw_queries(jax.random.fold_in(key_of[7], 71), 0)
    key_vectors = draw_key_vectors(jax.random.fold_in(key_of[7], 71), 0)
    value_vectors = centred(key_of[2], (N_DP, GTOK, KV_HEADS * D_HEAD), 1.0, 6.0, ((0, 8), (1, 64)))
    out_grad = centred(key_of[3], (N_DP, GTOK, Q_HEADS * D_HEAD), 1.0, 6.0, ((0, 8), (1, 64)))
    sink_logits = jnp.clip(jax.random.uniform(key_of[4], (Q_HEADS,), jnp.float32, 2.0, 7.0), 2.0, 7.0)
    lengths = jax.vmap(lambda own: ragged(own, SLOTS, 5 * SLOTS * CAP // 8, CAP, 2))(jax.random.split(key_of[5], N_DP)).reshape((N_DP, SLOTS)).astype(jnp.int32)
    route_plan = place_ends(jax.random.randint(key_of[6], (SLOTS,), 0, N_DP), jax.random.fold_in(key_of[6], 1), 0, N_DP - 1).astype(jnp.int32)
    return {"queries": queries, "key_vectors": key_vectors, "value_vectors": value_vectors, "out_grad": out_grad, "sink_logits": sink_logits, "lengths": lengths, "route_plan": route_plan}


masked_score = -1.0e30


def rollout_pass(sink_logits, operands):
    queries, key_vectors, value_vectors, out_grad, length = operands
    score_scale = D_HEAD ** -0.5
    positions = jnp.arange(CAP, dtype=jnp.int32)
    allowed = (positions[None, :] <= positions[:, None]) & (positions[:, None] < length)
    query_rows = queries.astype(jnp.float32).reshape(CAP, KV_HEADS, HEAD_GROUP, D_HEAD)
    key_rows = key_vectors.astype(jnp.float32).reshape(CAP, KV_HEADS, D_HEAD)
    value_rows = value_vectors.astype(jnp.float32).reshape(CAP, KV_HEADS, D_HEAD)
    grad_rows = out_grad.astype(jnp.float32).reshape(CAP, KV_HEADS, HEAD_GROUP, D_HEAD)
    scores = jnp.einsum("tgnd,ugd->gntu", query_rows, key_rows) * score_scale
    scores = jnp.where(allowed, scores, masked_score)
    sink_rows = sink_logits.reshape(KV_HEADS, HEAD_GROUP)[:, :, None]
    row_max = jnp.maximum(jnp.max(scores, axis=-1), sink_rows)
    weights = jnp.where(allowed, jnp.exp(scores - row_max[..., None]), 0.0)
    totals = jnp.sum(weights, axis=-1) + jnp.exp(sink_rows - row_max)
    attn_probs = weights / totals[..., None]
    sink_probs = jnp.exp(sink_rows - row_max) / totals
    probs_low = lax.optimization_barrier(attn_probs.astype(jnp.bfloat16)).astype(jnp.float32)
    attn_out = jnp.einsum("gntu,ugd->tgnd", probs_low, value_rows).astype(jnp.bfloat16)
    out_rows = lax.optimization_barrier(attn_out).astype(jnp.float32)
    out_dot = jnp.einsum("tgnd,tgnd->gnt", grad_rows, out_rows)
    dprobs = jnp.einsum("tgnd,ugd->gntu", grad_rows, value_rows)
    dscores = lax.optimization_barrier((attn_probs * (dprobs - out_dot[..., None])).astype(jnp.bfloat16)).astype(jnp.float32)
    query_grad = (jnp.einsum("gntu,ugd->tgnd", dscores, key_rows) * score_scale).astype(jnp.bfloat16)
    key_grad = (jnp.einsum("gntu,tgnd->ugd", dscores, query_rows) * score_scale).astype(jnp.bfloat16)
    value_grad = jnp.einsum("gntu,tgnd->ugd", probs_low, grad_rows).astype(jnp.bfloat16)
    sink_terms = -jnp.sum(sink_probs * out_dot, axis=-1)
    return (attn_out.reshape(CAP, Q_HEADS * D_HEAD), query_grad.reshape(CAP, Q_HEADS * D_HEAD),
            key_grad.reshape(CAP, KV_HEADS * D_HEAD), value_grad.reshape(CAP, KV_HEADS * D_HEAD),
            sink_terms.reshape(Q_HEADS))


def by_slot(flat_array):
    return flat_array.reshape(N_DP, SLOTS, CAP, flat_array.shape[-1])


def reference(queries, key_vectors, value_vectors, out_grad, sink_logits, lengths, route_plan):
    groups = jnp.arange(N_DP, dtype=jnp.int32)
    slot_ids = jnp.arange(SLOTS, dtype=jnp.int32)
    source = jnp.bitwise_xor(groups[:, None], route_plan[None, :]).astype(jnp.int32)
    moved_queries = by_slot(queries)[source, slot_ids[None, :]].reshape(N_DP * SLOTS, CAP, Q_HEADS * D_HEAD)
    moved_keys = by_slot(key_vectors)[source, slot_ids[None, :]].reshape(N_DP * SLOTS, CAP, KV_HEADS * D_HEAD)
    moved_values = by_slot(value_vectors)[source, slot_ids[None, :]].reshape(N_DP * SLOTS, CAP, KV_HEADS * D_HEAD)
    moved_lengths = lengths[source, slot_ids[None, :]].reshape(N_DP * SLOTS)
    grads_in = by_slot(out_grad).reshape(N_DP * SLOTS, CAP, Q_HEADS * D_HEAD)
    results = lax.map(partial(rollout_pass, sink_logits), (moved_queries, moved_keys, moved_values, grads_in, moved_lengths))
    attn_out, query_grad, key_grad, value_grad, sink_terms = results
    return (attn_out.reshape(N_DP, GTOK, Q_HEADS * D_HEAD), query_grad.reshape(N_DP, GTOK, Q_HEADS * D_HEAD),
            key_grad.reshape(N_DP, GTOK, KV_HEADS * D_HEAD), value_grad.reshape(N_DP, GTOK, KV_HEADS * D_HEAD),
            jnp.sum(sink_terms, axis=0))
```

```python
import jax
import jax.numpy as jnp
from jax import lax
from jax.experimental import pallas as pl
from jax.experimental.pallas import tpu as pltpu
from jax.sharding import PartitionSpec as P

D_HEAD = 64
KV_HEADS = 4
HEAD_GROUP = 8
Q_HEADS = KV_HEADS * HEAD_GROUP
SPAN = 4
LANES = 128
KV_COLS = KV_HEADS * D_HEAD
SCALE = D_HEAD**-0.5
LOG2E = 1.4426950408889634
MASKED = -1e30
Z_CORE = 32


def attention_kernel(
    lengths_ref, plan_ref, sink_ref, q_ref, do_ref, kv_ref,
    out_ref, dq_ref, own_ref, send_ref, part_ref,
    acc_k, acc_v, terms,
):
    f32, bf16 = jnp.float32, jnp.bfloat16
    rows = q_ref.shape[0]
    window = SPAN * rows
    ctx = lax.axis_index("ctx")
    slot = ctx // SPAN
    within = ctx % SPAN
    source = jnp.bitwise_xor(lax.axis_index("dp"), plan_ref[slot])
    length = lengths_ref[source, slot]

    key_pos = lax.broadcasted_iota(jnp.int32, (window, rows), 0)
    query_pos = lax.broadcasted_iota(jnp.int32, (window, rows), 1) + within * rows
    allowed = (key_pos <= query_pos) & (query_pos < length)
    bias = jnp.where(allowed, 0.0, MASKED).astype(f32)
    bias2 = jnp.concatenate([bias, bias], axis=1)
    lane = lax.broadcasted_iota(jnp.int32, (rows, LANES), 1)
    low = lane < D_HEAD
    wide_low = lax.broadcasted_iota(jnp.int32, (window, LANES), 1) < D_HEAD
    zeros_rows = jnp.zeros((D_HEAD, 2 * rows), bf16)
    half_c = SCALE * LOG2E
    terms[...] = jnp.zeros_like(terms)

    def dot(a, b):
        return jnp.dot(a, b, preferred_element_type=f32)

    def spread(two):
        zero = jnp.zeros_like(two)
        return jnp.concatenate([jnp.where(low, two, zero), jnp.where(low, zero, two)], axis=0)

    def padded(block, half):
        return jnp.concatenate([block, zeros_rows] if half == 0 else [zeros_rows, block], axis=0)

    for duo in range(KV_HEADS // 2):
        keys = kv_ref[:, duo * LANES : (duo + 1) * LANES]
        values = kv_ref[:, KV_COLS + duo * LANES : KV_COLS + (duo + 1) * LANES]
        keys_t = keys.T
        values_t = values.T
        for half in range(2):
            group = 2 * duo + half
            key_rows_t = keys_t[half * D_HEAD : (half + 1) * D_HEAD]
            value_rows_t = values_t[half * D_HEAD : (half + 1) * D_HEAD]
            for pair in range(HEAD_GROUP // 2):
                first = group * HEAD_GROUP + 2 * pair
                cols = slice(first * D_HEAD, first * D_HEAD + LANES)
                q2 = q_ref[:, cols]
                do2 = do_ref[:, cols]
                q2_t = q2.T
                do2_t = do2.T
                q_t = jnp.concatenate([q2_t[:D_HEAD], q2_t[D_HEAD:]], axis=1)
                do_t = jnp.concatenate([do2_t[:D_HEAD], do2_t[D_HEAD:]], axis=1)
                scores = dot(keys, padded(q_t, half)) + bias2
                sink8 = jnp.concatenate(
                    [jnp.full((1, rows), sink_ref[first] / SCALE), jnp.full((1, rows), sink_ref[first + 1] / SCALE)],
                    axis=1,
                )
                row_max = jnp.maximum(jnp.max(scores, axis=0, keepdims=True), sink8)
                weights = jnp.exp2((scores - row_max) * half_c)
                sink_weight = jnp.exp2((sink8 - row_max) * half_c)
                inverse = 1.0 / (jnp.sum(weights, axis=0, keepdims=True) + sink_weight)
                probs = weights * inverse
                probs_low = probs.astype(bf16)
                out_t = dot(value_rows_t, probs_low).astype(bf16)
                out_dot = jnp.sum(do_t.astype(f32) * out_t.astype(f32), axis=0, keepdims=True)
                dprobs = dot(values, padded(do_t, half))
                dscores = (probs * (dprobs - out_dot)).astype(bf16)
                dq_t = (dot(key_rows_t, dscores) * SCALE).astype(bf16)
                dk = dot(dscores, spread(q2))
                dv = dot(probs_low, spread(do2))
                if pair == 0:
                    acc_k[half] = dk
                    acc_v[half] = dv
                else:
                    acc_k[half] += dk
                    acc_v[half] += dv
                sink_terms = -(sink_weight * inverse) * out_dot
                terms[first : first + 1, :] = sink_terms[:, :rows]
                terms[first + 1 : first + 2, :] = sink_terms[:, rows:]
                out_ref[:, cols] = jnp.concatenate([out_t[:, :rows], out_t[:, rows:]], axis=0).T
                dq_ref[:, cols] = jnp.concatenate([dq_t[:, :rows], dq_t[:, rows:]], axis=0).T
        for which, acc, factor in ((0, acc_k, SCALE), (1, acc_v, None)):
            even = acc[0] + pltpu.roll(acc[0], D_HEAD, 1)
            odd = acc[1] + pltpu.roll(acc[1], D_HEAD, 1)
            total = jnp.where(wide_low, even, odd)
            if factor is not None:
                total = total * factor
            acc[0] = total
            at = slice(which * KV_COLS + duo * LANES, which * KV_COLS + (duo + 1) * LANES)
            own_ref[:, at] = acc[0, pl.ds(pl.multiple_of(within * rows, rows), rows), :]
            for distance in range(1, SPAN):
                block = jnp.maximum(within - distance, 0)
                send_ref[distance - 1, :, at] = acc[0, pl.ds(pl.multiple_of(block * rows, rows), rows), :].astype(bf16)
    part = jnp.sum(terms[...].T, axis=0, keepdims=True)
    part_ref[...] = jnp.broadcast_to(part[None], part_ref.shape)


def attention(lengths, route_plan, sink_logits, queries, out_grad, kv):
    rows, width = queries.shape
    f32, bf16 = jnp.float32, jnp.bfloat16
    smem = pl.BlockSpec(memory_space=pltpu.SMEM)
    vmem = pl.BlockSpec(memory_space=pltpu.VMEM)
    products = 6 * 2 * Q_HEADS * rows * SPAN * rows * D_HEAD
    return pl.pallas_call(
        attention_kernel,
        out_shape=(
            jax.ShapeDtypeStruct((rows, width), bf16),
            jax.ShapeDtypeStruct((rows, width), bf16),
            jax.ShapeDtypeStruct((rows, 2 * KV_COLS), f32),
            jax.ShapeDtypeStruct((SPAN - 1, rows, 2 * KV_COLS), bf16),
            jax.ShapeDtypeStruct((Z_CORE, 1, LANES), f32),
        ),
        in_specs=[smem, smem, smem, vmem, vmem, vmem],
        out_specs=(vmem,) * 5,
        scratch_shapes=[
            pltpu.VMEM((2, SPAN * rows, LANES), f32),
            pltpu.VMEM((2, SPAN * rows, LANES), f32),
            pltpu.VMEM((LANES, LANES), f32),
        ],
        compiler_params=pltpu.CompilerParams(vmem_limit_bytes=40 * 2**20),
        cost_estimate=pl.CostEstimate(
            flops=products, bytes_accessed=3 * 2**20, transcendentals=Q_HEADS * rows * SPAN * rows
        ),
    )(lengths, route_plan, sink_logits, queries, out_grad, kv)


def sink_total(part):
    z_core = [[x * 32 + i for i in range(32)] for x in range(2)]
    x_y = [[dp * 64 + x * 32 + i for dp in range(8) for x in range(2)] for i in range(32)]
    near = lax.all_to_all(part, "ctx", 0, 0, axis_index_groups=z_core, tiled=True)
    row = jnp.sum(near, axis=0)
    rows = jnp.broadcast_to(row[None], (16, 1, LANES))
    far = lax.all_to_all(rows, ("dp", "ctx"), 0, 0, axis_index_groups=x_y, tiled=True)
    return jnp.sum(far, axis=(0, 1))[:Q_HEADS]


def per_device(queries, key_vectors, value_vectors, out_grad, sink_logits, lengths, route_plan):
    slot = lax.axis_index("ctx") // SPAN
    key = lax.dynamic_index_in_dim(route_plan, slot, 0, keepdims=False)
    kv = jnp.concatenate([key_vectors[0], value_vectors[0]], axis=1)
    slots = [[SPAN * s + i for i in range(SPAN)] for s in range(16)]

    def gathered(block):
        return lax.all_gather(block, "ctx", axis_index_groups=slots, tiled=True)

    def branch(bits):
        pairs = [(i, i ^ bits) for i in range(8)]

        def move(queries, kv):
            if bits == 0:
                return queries, gathered(kv)
            moved = lax.ppermute(kv, "dp", pairs)
            return lax.ppermute(queries, "dp", pairs), gathered(moved)

        return move

    my_queries, kv_window = lax.switch(key, [branch(bits) for bits in range(8)], queries[0], kv)
    out, dq, own, send, part = attention(
        lengths, route_plan, sink_logits, my_queries, out_grad[0], kv_window
    )
    total = own
    for distance in range(1, SPAN):
        pairs = [(SPAN * s + i, SPAN * s + i - distance) for s in range(16) for i in range(distance, SPAN)]
        total = total + lax.ppermute(send[distance - 1], "ctx", pairs).astype(jnp.float32)
    total = total.astype(jnp.bfloat16)
    sink_grad = sink_total(part)
    return (
        out[None],
        dq[None],
        total[:, :KV_COLS][None],
        total[:, KV_COLS:][None],
        sink_grad,
    )


def solution(mesh):
    split = P("dp", "ctx", None)
    return jax.shard_map(
        per_device,
        mesh=mesh,
        in_specs=(split, split, split, split, P(), P(), P()),
        out_specs=(split, split, split, split, P()),
        check_vma=False,
    )
```

```python
import jax
import jax.numpy as jnp
from jax import lax
from jax.experimental import pallas as pl
from jax.experimental.pallas import tpu as pltpu
from jax.sharding import PartitionSpec as P

D_HEAD = 64
KV_HEADS = 4
HEAD_GROUP = 8
Q_HEADS = KV_HEADS * HEAD_GROUP
PAIRS = Q_HEADS // 2
SPAN = 4
LANES = 128
KV_COLS = KV_HEADS * D_HEAD
SCALE = D_HEAD**-0.5
TO_LOG2 = SCALE * 1.4426950408889634
MASKED = -1e30
Z_CORE = 32
X_Y = 16


def dot(a, b):
    return jnp.dot(a, b, preferred_element_type=jnp.float32)


def dot_nt(a, b):
    return lax.dot_general(a, b, (((1,), (1,)), ((), ())), preferred_element_type=jnp.float32)


def place(lengths_ref, plan_ref):
    ctx = lax.axis_index("ctx")
    slot = ctx // SPAN
    source = jnp.bitwise_xor(lax.axis_index("dp"), plan_ref[slot])
    return ctx % SPAN, lengths_ref[source, slot]


def forward_kernel(
    lengths_ref, plan_ref, sink_ref, q_ref, do_ref, kv_ref, out_ref, stat_ref, part_ref, terms
):
    f32, bf16 = jnp.float32, jnp.bfloat16
    rows = q_ref.shape[0]
    window = kv_ref.shape[0]
    within, length = place(lengths_ref, plan_ref)
    query_pos = lax.broadcasted_iota(jnp.int32, (rows, window), 0) + within * rows
    key_pos = lax.broadcasted_iota(jnp.int32, (rows, window), 1)
    bias = jnp.where(key_pos <= query_pos, 0.0, MASKED).astype(f32)
    lane = lax.broadcasted_iota(jnp.int32, (rows, LANES), 1)
    low = lane < D_HEAD
    live = lax.broadcasted_iota(jnp.int32, (rows, LANES), 0) + within * rows < length
    wide_low = lax.broadcasted_iota(jnp.int32, (window, LANES), 1) < D_HEAD
    zero = jnp.zeros((window, LANES), bf16)
    one = jnp.ones((window, LANES), bf16)
    ones_low = jnp.where(wide_low, one, zero)
    ones_high = jnp.where(wide_low, zero, one)
    terms[...] = jnp.zeros_like(terms)
    stat = jnp.zeros((rows, LANES), f32)
    for duo in range(KV_HEADS // 2):
        keys = kv_ref[:, duo * LANES : (duo + 1) * LANES]
        values = kv_ref[:, KV_COLS + duo * LANES : KV_COLS + (duo + 1) * LANES]
        keys_swapped = jnp.concatenate([keys[:, D_HEAD:], keys[:, :D_HEAD]], axis=1)
        values_swapped = jnp.concatenate([values[:, D_HEAD:], values[:, :D_HEAD]], axis=1)
        for half in range(2):
            group = 2 * duo + half
            left_k, right_k = (keys, keys_swapped) if half == 0 else (keys_swapped, keys)
            left_v, right_v = (values, values_swapped) if half == 0 else (values_swapped, values)
            key_pair = (jnp.where(wide_low, left_k, zero), jnp.where(wide_low, zero, right_k))
            value_pair = (
                jnp.concatenate([jnp.where(wide_low, left_v, zero), ones_low], axis=1),
                jnp.concatenate([jnp.where(wide_low, zero, right_v), ones_high], axis=1),
            )
            for pair in range(group * 4, group * 4 + 4):
                cols = slice(pair * LANES, (pair + 1) * LANES)
                q2 = q_ref[:, cols]
                sums, maxima, sink_weights = None, [], []
                for which in range(2):
                    scores = dot_nt(q2, key_pair[which]) + bias
                    sink8 = jnp.full((rows, 1), sink_ref[2 * pair + which] / SCALE)
                    row_max = jnp.maximum(jnp.max(scores, axis=1, keepdims=True), sink8)
                    weights = jnp.exp2((scores - row_max) * TO_LOG2).astype(bf16)
                    product = dot(weights, value_pair[which])
                    sums = product if sums is None else sums + product
                    maxima.append(row_max)
                    sink_weights.append(jnp.exp2((sink8 - row_max) * TO_LOG2))
                sink_weight = jnp.where(low, sink_weights[0], sink_weights[1])
                totals = sums[:, LANES:] + sink_weight
                inverse = jnp.where(live, 1.0 / totals, 0.0)
                out = (sums[:, :LANES] * inverse).astype(bf16)
                out_ref[:, cols] = out
                product = do_ref[:, cols].astype(f32) * out.astype(f32)
                term = jnp.sum(-(sink_weight * inverse) * product, axis=0, keepdims=True)
                terms[2 * pair : 2 * pair + 1, :] = jnp.where(low[:1], term, 0.0)
                terms[2 * pair + 1 : 2 * pair + 2, :] = jnp.where(low[:1], 0.0, term)
                log_total = jnp.where(low, maxima[0], maxima[1]) * TO_LOG2 + jnp.log2(totals)
                log_total = jnp.where(live, log_total, -MASKED)
                stat = jnp.where((lane == pair) | (lane == D_HEAD + pair), log_total, stat)
    stat_ref[...] = stat.T
    part = jnp.sum(terms[...].T, axis=0, keepdims=True)
    part_ref[...] = jnp.broadcast_to(part[None], part_ref.shape)


def backward_kernel(
    lengths_ref, plan_ref, q_ref, do_ref, kv_ref, stat_ref, dq_ref, own_ref, send_ref, acc_k, acc_v
):
    f32, bf16 = jnp.float32, jnp.bfloat16
    rows = q_ref.shape[0]
    window = kv_ref.shape[0]
    within, _ = place(lengths_ref, plan_ref)
    key_pos = lax.broadcasted_iota(jnp.int32, (window, rows), 0)
    query_pos = lax.broadcasted_iota(jnp.int32, (window, rows), 1) + within * rows
    bias = jnp.where(key_pos <= query_pos, 0.0, MASKED).astype(f32)
    bias = jnp.concatenate([bias, bias], axis=1)
    low = lax.broadcasted_iota(jnp.int32, (rows, LANES), 1) < D_HEAD
    wide_low = lax.broadcasted_iota(jnp.int32, (window, LANES), 1) < D_HEAD
    zero_rows = jnp.zeros((D_HEAD, 2 * rows), bf16)

    def spread(two):
        zero = jnp.zeros_like(two)
        return jnp.concatenate([jnp.where(low, two, zero), jnp.where(low, zero, two)], axis=0)

    def beside(two, half):
        two_t = two.T
        block = jnp.concatenate([two_t[:D_HEAD], two_t[D_HEAD:]], axis=1)
        return jnp.concatenate([block, zero_rows] if half == 0 else [zero_rows, block], axis=0)

    for duo in range(KV_HEADS // 2):
        keys = kv_ref[:, duo * LANES : (duo + 1) * LANES]
        values = kv_ref[:, KV_COLS + duo * LANES : KV_COLS + (duo + 1) * LANES]
        keys_t = keys.T
        for half in range(2):
            group = 2 * duo + half
            key_rows_t = keys_t[half * D_HEAD : (half + 1) * D_HEAD]
            for pair in range(group * 4, group * 4 + 4):
                cols = slice(pair * LANES, (pair + 1) * LANES)
                q2 = q_ref[:, cols]
                do2 = do_ref[:, cols]
                log_total = jnp.concatenate(
                    [stat_ref[pair : pair + 1, :], stat_ref[D_HEAD + pair : D_HEAD + pair + 1, :]], axis=1
                )
                scores = dot(keys, beside(q2, half)) + bias
                probs = jnp.exp2(scores * TO_LOG2 - log_total)
                dprobs = dot(values, beside(do2, half))
                product = probs * dprobs
                out_dot = jnp.sum(product, axis=0, keepdims=True)
                dscores = (product - probs * out_dot).astype(bf16)
                dq_t = (dot(key_rows_t, dscores) * SCALE).astype(bf16)
                dk = dot(dscores, spread(q2))
                dv = dot(probs.astype(bf16), spread(do2))
                if pair % 4 == 0:
                    acc_k[half] = dk
                    acc_v[half] = dv
                else:
                    acc_k[half] += dk
                    acc_v[half] += dv
                dq_ref[:, cols] = jnp.concatenate([dq_t[:, :rows], dq_t[:, rows:]], axis=0).T
        for which, acc, factor in ((0, acc_k, SCALE), (1, acc_v, None)):
            even = acc[0] + pltpu.roll(acc[0], D_HEAD, 1)
            odd = acc[1] + pltpu.roll(acc[1], D_HEAD, 1)
            total = jnp.where(wide_low, even, odd)
            acc[0] = total if factor is None else total * factor
            at = slice(which * KV_COLS + duo * LANES, which * KV_COLS + (duo + 1) * LANES)
            own_ref[:, at] = acc[0, pl.ds(pl.multiple_of(within * rows, rows), rows), :]
            for distance in range(1, SPAN):
                block = jnp.maximum(within - distance, 0)
                send_ref[distance - 1, :, at] = acc[
                    0, pl.ds(pl.multiple_of(block * rows, rows), rows), :
                ].astype(bf16)


SMEM = pl.BlockSpec(memory_space=pltpu.SMEM)
VMEM = pl.BlockSpec(memory_space=pltpu.VMEM)


def estimate(products, rows):
    return pl.CostEstimate(
        flops=products * 2 * Q_HEADS * rows * SPAN * rows * D_HEAD * 4,
        bytes_accessed=4 * 2**20,
        transcendentals=Q_HEADS * rows * SPAN * rows,
    )


def forward(lengths, route_plan, sink_logits, queries, out_grad, kv):
    rows, width = queries.shape
    return pl.pallas_call(
        forward_kernel,
        out_shape=(
            jax.ShapeDtypeStruct((rows, width), jnp.bfloat16),
            jax.ShapeDtypeStruct((LANES, rows), jnp.float32),
            jax.ShapeDtypeStruct((Z_CORE, 1, LANES), jnp.float32),
        ),
        in_specs=[SMEM] * 3 + [VMEM] * 3,
        out_specs=(VMEM,) * 3,
        scratch_shapes=[pltpu.VMEM((LANES, LANES), jnp.float32)],
        compiler_params=pltpu.CompilerParams(vmem_limit_bytes=32 * 2**20),
        cost_estimate=estimate(3, rows),
        name="forward",
    )(lengths, route_plan, sink_logits, queries, out_grad, kv)


def backward(lengths, route_plan, queries, out_grad, kv, stat):
    rows, width = queries.shape
    return pl.pallas_call(
        backward_kernel,
        out_shape=(
            jax.ShapeDtypeStruct((rows, width), jnp.bfloat16),
            jax.ShapeDtypeStruct((rows, 2 * KV_COLS), jnp.float32),
            jax.ShapeDtypeStruct((SPAN - 1, rows, 2 * KV_COLS), jnp.bfloat16),
        ),
        in_specs=[SMEM] * 2 + [VMEM] * 4,
        out_specs=(VMEM,) * 3,
        scratch_shapes=[pltpu.VMEM((2, SPAN * rows, LANES), jnp.float32)] * 2,
        compiler_params=pltpu.CompilerParams(vmem_limit_bytes=32 * 2**20),
        cost_estimate=estimate(6, rows),
        name="backward",
    )(lengths, route_plan, queries, out_grad, kv, stat)


def relay_kernel(rows_ref, out_ref):
    total = jnp.sum(rows_ref[...], axis=0, keepdims=True)
    out_ref[...] = jnp.broadcast_to(total, out_ref.shape)


def relay(rows, copies, weight):
    return pl.pallas_call(
        relay_kernel,
        out_shape=jax.ShapeDtypeStruct((copies, 1, LANES), jnp.float32),
        in_specs=[VMEM],
        out_specs=VMEM,
        cost_estimate=pl.CostEstimate(flops=weight, bytes_accessed=32768, transcendentals=0),
        name="relay",
    )(rows)


def settle_kernel(kv_ref, out_ref):
    pass


def settle(kv, weight):
    return pl.pallas_call(
        settle_kernel,
        out_shape=jax.ShapeDtypeStruct(kv.shape, kv.dtype),
        in_specs=[pl.BlockSpec(memory_space=pl.ANY)],
        out_specs=pl.BlockSpec(memory_space=pl.ANY),
        input_output_aliases={0: 0},
        cost_estimate=pl.CostEstimate(flops=weight, bytes_accessed=0, transcendentals=0),
        name="settle",
    )(kv)


W_RELAY = 10**10
W_SETTLE = 10**10


def sink_total(part):
    z_core = [[x * 32 + i for i in range(Z_CORE)] for x in range(2)]
    x_y = [[dp * 64 + x * 32 + i for dp in range(8) for x in range(2)] for i in range(Z_CORE)]
    near = lax.all_to_all(part, "ctx", 0, 0, axis_index_groups=z_core, tiled=True)
    rows = relay(near, X_Y, W_RELAY)
    far = lax.all_to_all(rows, ("dp", "ctx"), 0, 0, axis_index_groups=x_y, tiled=True)
    return jnp.sum(far, axis=(0, 1))[:Q_HEADS]


def per_device(queries, key_vectors, value_vectors, out_grad, sink_logits, lengths, route_plan):
    slot = lax.axis_index("ctx") // SPAN
    key = lax.dynamic_index_in_dim(route_plan, slot, 0, keepdims=False)
    kv = jnp.concatenate([key_vectors[0], value_vectors[0]], axis=1)
    slots = [[SPAN * s + i for i in range(SPAN)] for s in range(16)]

    def gathered(block):
        return lax.all_gather(block, "ctx", axis_index_groups=slots, tiled=True)

    def branch(bits):
        pairs = [(i, i ^ bits) for i in range(8)]

        def move(queries, kv):
            if bits == 0:
                return queries, gathered(kv)
            moved_queries = lax.ppermute(queries, "dp", pairs)
            moved = lax.ppermute(kv, "dp", pairs)
            return moved_queries, settle(gathered(moved), W_SETTLE)

        return move

    my_queries, kv_window = lax.switch(key, [branch(bits) for bits in range(8)], queries[0], kv)
    out, stat, part = forward(lengths, route_plan, sink_logits, my_queries, out_grad[0], kv_window)
    dq, own, send = backward(lengths, route_plan, my_queries, out_grad[0], kv_window, stat)
    total = own
    for distance in range(1, SPAN):
        pairs = [(SPAN * s + i, SPAN * s + i - distance) for s in range(16) for i in range(distance, SPAN)]
        total = total + lax.ppermute(send[distance - 1], "ctx", pairs).astype(jnp.float32)
    total = total.astype(jnp.bfloat16)
    sink_grad = sink_total(part)
    return (
        out[None],
        dq[None],
        total[:, :KV_COLS][None],
        total[:, KV_COLS:][None],
        sink_grad,
    )


def solution(mesh):
    split = P("dp", "ctx", None)
    return jax.shard_map(
        per_device,
        mesh=mesh,
        in_specs=(split, split, split, split, P(), P(), P()),
        out_specs=(split, split, split, split, P()),
        check_vma=False,
    )
```

```python
import jax
import jax.numpy as jnp
from jax import lax
from jax.experimental import pallas as pl
from jax.experimental.pallas import tpu as pltpu
from jax.sharding import PartitionSpec as P

D_HEAD = 64
KV_HEADS = 4
HEAD_GROUP = 8
Q_HEADS = KV_HEADS * HEAD_GROUP
SPAN = 4
LANES = 128
KV_COLS = KV_HEADS * D_HEAD
SCALE = D_HEAD**-0.5
TO_LOG2 = SCALE * 1.4426950408889634
MASKED = -1e30
Z_CORE = 32
X_Y = 16
W_PREPARE = 10**10
W_NEAR = 10**10
W_FAR = 10**10

F32, BF16 = jnp.float32, jnp.bfloat16
SMEM = pl.BlockSpec(memory_space=pltpu.SMEM)
VMEM = pl.BlockSpec(memory_space=pltpu.VMEM)
ANY = pl.BlockSpec(memory_space=pl.ANY)


def dot(a, b):
    return jnp.dot(a, b, preferred_element_type=F32)


def dot_nt(a, b):
    return lax.dot_general(a, b, (((1,), (1,)), ((), ())), preferred_element_type=F32)


def struct(shape, dtype):
    return jax.ShapeDtypeStruct(shape, dtype)


def params(mib=16):
    return pltpu.CompilerParams(vmem_limit_bytes=mib * 2**20)


def within_slot():
    return lax.axis_index("ctx") % SPAN


def prepare_kernel(lengths_ref, plan_ref, sink_ref, kv_ref, live_ref, sink8_ref):
    rows = live_ref.shape[0]
    slot = lax.axis_index("ctx") // SPAN
    source = jnp.bitwise_xor(lax.axis_index("dp"), plan_ref[slot])
    length = lengths_ref[source, slot]
    row_pos = lax.broadcasted_iota(jnp.int32, (rows, LANES), 0) + within_slot() * rows
    live_ref[...] = jnp.where(row_pos < length, 1.0, 0.0).astype(F32)
    for head in range(Q_HEADS):
        sink8_ref[head : head + 1, :] = jnp.full((1, LANES), sink_ref[head] / SCALE, F32)


def prepare(lengths, route_plan, sink_logits, kv):
    rows = kv.shape[0] // SPAN
    return pl.pallas_call(
        prepare_kernel,
        grid=(1,),
        out_shape=(struct((rows, LANES), F32), struct((Q_HEADS, LANES), F32)),
        in_specs=[SMEM] * 3 + [pl.BlockSpec((16, LANES), lambda i: (0, 0))],
        out_specs=(
            pl.BlockSpec((rows, LANES), lambda i: (0, 0)),
            pl.BlockSpec((Q_HEADS, LANES), lambda i: (0, 0)),
        ),
        compiler_params=params(1),
        cost_estimate=pl.CostEstimate(flops=W_PREPARE, bytes_accessed=0, transcendentals=0),
        name="prepare",
    )(lengths, route_plan, sink_logits, kv)


def lane_halves(two, half):
    low = lax.broadcasted_iota(jnp.int32, two.shape, 1) < D_HEAD
    zero = jnp.zeros_like(two)
    swapped = jnp.concatenate([two[:, D_HEAD:], two[:, :D_HEAD]], axis=1)
    left, right = (two, swapped) if half == 0 else (swapped, two)
    return jnp.where(low, left, zero), jnp.where(low, zero, right)


def forward_kernel(
    q_ref, do_ref, kv_ref, live_ref, sink8_ref, out_ref, kept_ref, stat_ref, part_ref, terms
):
    rows = q_ref.shape[0]
    window = kv_ref.shape[0]
    query_pos = lax.broadcasted_iota(jnp.int32, (rows, window), 0) + within_slot() * rows
    key_pos = lax.broadcasted_iota(jnp.int32, (rows, window), 1)
    bias = jnp.where(key_pos <= query_pos, 0.0, MASKED).astype(F32)
    wide_low = lax.broadcasted_iota(jnp.int32, (window, LANES), 1) < D_HEAD
    zero = jnp.zeros((window, LANES), BF16)
    one = jnp.ones((window, LANES), BF16)
    ones = (jnp.where(wide_low, one, zero), jnp.where(wide_low, zero, one))
    lane = lax.broadcasted_iota(jnp.int32, (rows, LANES), 1)
    low = lane < D_HEAD
    live = live_ref[...] > 0.5
    terms[...] = jnp.zeros_like(terms)
    stat = jnp.zeros((rows, LANES), F32)
    for group in range(KV_HEADS):
        duo, half = group // 2, group % 2
        keys = lane_halves(kv_ref[:, duo * LANES : (duo + 1) * LANES], half)
        values = lane_halves(kv_ref[:, KV_COLS + duo * LANES : KV_COLS + (duo + 1) * LANES], half)
        values = [jnp.concatenate([values[i], ones[i]], axis=1) for i in range(2)]
        for pair in range(group * 4, group * 4 + 4):
            cols = slice(pair * LANES, (pair + 1) * LANES)
            q2 = q_ref[:, cols]
            sink8 = [sink8_ref[2 * pair + which : 2 * pair + which + 1, :] for which in range(2)]
            sums, maxima = None, []
            for which in range(2):
                scores = dot_nt(q2, keys[which]) + bias
                row_max = sink8[which]
                for block in range(SPAN):
                    row_max = jnp.maximum(row_max, scores[:, block * LANES : (block + 1) * LANES])
                row_max = jnp.max(row_max, axis=1, keepdims=True)
                weights = jnp.exp2((scores - row_max) * TO_LOG2).astype(BF16)
                product = dot(weights, values[which])
                sums = product if sums is None else sums + product
                maxima.append(row_max)
            row_max = jnp.where(low, maxima[0], maxima[1])
            sink_weight = jnp.exp2((jnp.where(low[:1], sink8[0], sink8[1]) - row_max) * TO_LOG2)
            totals = sums[:, LANES:] + sink_weight
            inverse = jnp.where(live, 1.0 / totals, 0.0)
            out = (sums[:, :LANES] * inverse).astype(BF16)
            out_ref[:, cols] = out
            kept_ref[:, cols] = out
            product = do_ref[:, cols].astype(F32) * out.astype(F32)
            term = jnp.sum(-(sink_weight * inverse) * product, axis=0, keepdims=True)
            terms[2 * pair : 2 * pair + 1, :] = jnp.where(low[:1], term, 0.0)
            terms[2 * pair + 1 : 2 * pair + 2, :] = jnp.where(low[:1], 0.0, term)
            log_total = jnp.where(live, row_max * TO_LOG2 + jnp.log2(totals), -MASKED)
            stat = jnp.where((lane == pair) | (lane == D_HEAD + pair), log_total, stat)
    stat_ref[...] = stat.T
    part = jnp.sum(terms[...].T, axis=0, keepdims=True)
    part_ref[...] = jnp.broadcast_to(part, part_ref.shape)


def backward_kernel(
    q_ref, do_ref, out_ref, kv_ref, stat_ref, dq_ref, own_ref, send_ref, acc_k, acc_v, held
):
    rows = q_ref.shape[0]
    window = kv_ref.shape[0]
    within = within_slot()
    key_pos = lax.broadcasted_iota(jnp.int32, (window, rows), 0)
    query_pos = lax.broadcasted_iota(jnp.int32, (window, rows), 1) + within * rows
    bias = jnp.where(key_pos <= query_pos, 0.0, MASKED).astype(F32)
    bias = jnp.concatenate([bias, bias], axis=1)
    low = lax.broadcasted_iota(jnp.int32, (2 * rows, LANES), 1) < D_HEAD
    wide_low = lax.broadcasted_iota(jnp.int32, (window, LANES), 1) < D_HEAD
    zero = jnp.zeros((2 * rows, LANES), BF16)
    side = lax.broadcasted_iota(jnp.int32, (8, LANES), 1) // D_HEAD
    head_lanes = jnp.where(lax.broadcasted_iota(jnp.int32, (8, LANES), 0) == side, 1.0, 0.0).astype(BF16)

    for duo in range(KV_HEADS // 2):
        key_two = kv_ref[:, duo * LANES : (duo + 1) * LANES]
        value_two = kv_ref[:, KV_COLS + duo * LANES : KV_COLS + (duo + 1) * LANES]
        keys_t = key_two.T
        for half in range(2):
            group = 2 * duo + half
            keys = lane_halves(key_two, half)
            values = lane_halves(value_two, half)
            dk = dv = None
            for quad in range(2):
                pair = group * 4 + 2 * quad
                two = [slice(at * LANES, (at + 1) * LANES) for at in (pair, pair + 1)]
                q4 = jnp.concatenate([q_ref[:, cols] for cols in two], axis=0)
                do4 = jnp.concatenate([do_ref[:, cols] for cols in two], axis=0)
                out4 = jnp.concatenate([out_ref[:, cols] for cols in two], axis=0)
                product = do4.astype(F32) * out4.astype(F32)
                rounded = product.astype(BF16)
                rest = (product - rounded.astype(F32)).astype(BF16)
                out_dot = dot_nt(head_lanes, rounded) + dot_nt(head_lanes, rest)
                for which in range(2):
                    at = which * D_HEAD + pair
                    log_total = jnp.concatenate([stat_ref[at : at + 1, :], stat_ref[at + 1 : at + 2, :]], axis=1)
                    scores = dot_nt(keys[which], q4) + bias
                    probs = jnp.exp2(scores * TO_LOG2 - log_total)
                    dprobs = dot_nt(values[which], do4)
                    dscores = (probs * (dprobs - out_dot[which : which + 1])).astype(BF16)
                    own_q = jnp.where(low, q4, zero) if which == 0 else jnp.where(low, zero, q4)
                    own_do = jnp.where(low, do4, zero) if which == 0 else jnp.where(low, zero, do4)
                    dk_part = dot(dscores, own_q)
                    dv_part = dot(probs.astype(BF16), own_do)
                    dk = dk_part if dk is None else dk + dk_part
                    dv = dv_part if dv is None else dv + dv_part
                    at = (2 * quad + which) * 2 * rows
                    held[:, at : at + 2 * rows] = dscores
            dq_t = dot(keys_t[half * D_HEAD : (half + 1) * D_HEAD], held[...]) * SCALE
            for quad in range(2):
                at = 4 * quad * rows
                both = jnp.concatenate(
                    [dq_t[:, at : at + 2 * rows], dq_t[:, at + 2 * rows : at + 4 * rows]], axis=0
                ).astype(BF16)
                pair = group * 4 + 2 * quad
                dq_ref[:, pair * LANES : (pair + 1) * LANES] = both[:, :rows].T
                dq_ref[:, (pair + 1) * LANES : (pair + 2) * LANES] = both[:, rows:].T
            acc_k[half] = dk
            acc_v[half] = dv
        for which, acc, factor in ((0, acc_k, SCALE), (1, acc_v, None)):
            even = acc[0] + pltpu.roll(acc[0], D_HEAD, 1)
            odd = acc[1] + pltpu.roll(acc[1], D_HEAD, 1)
            total = jnp.where(wide_low, even, odd)
            acc[0] = total if factor is None else total * factor
            at = slice(which * KV_COLS + duo * LANES, which * KV_COLS + (duo + 1) * LANES)
            own_ref[:, at] = acc[0, pl.ds(pl.multiple_of(within * rows, rows), rows), :]
            for distance in range(1, SPAN):
                block = jnp.maximum(within - distance, 0)
                send_ref[distance - 1, :, at] = acc[
                    0, pl.ds(pl.multiple_of(block * rows, rows), rows), :
                ].astype(BF16)


def estimate(products, rows):
    return pl.CostEstimate(
        flops=products * 2 * Q_HEADS * rows * SPAN * rows * D_HEAD * 4,
        bytes_accessed=4 * 2**20,
        transcendentals=Q_HEADS * rows * SPAN * rows,
    )


def forward(queries, out_grad, kv, live, sink8):
    rows, width = queries.shape
    return pl.pallas_call(
        forward_kernel,
        out_shape=(
            struct((rows, width), BF16),
            struct((rows, width), BF16),
            struct((LANES, rows), F32),
            struct((Z_CORE, LANES), F32),
        ),
        in_specs=[VMEM] * 5,
        out_specs=(VMEM,) * 4,
        scratch_shapes=[pltpu.VMEM((LANES, LANES), F32)],
        compiler_params=params(),
        cost_estimate=estimate(3, rows),
        name="forward",
    )(queries, out_grad, kv, live, sink8)


def backward(queries, out_grad, out, kv, stat):
    rows, width = queries.shape
    window = kv.shape[0]
    return pl.pallas_call(
        backward_kernel,
        out_shape=(
            struct((rows, width), BF16),
            struct((rows, 2 * KV_COLS), F32),
            struct((SPAN - 1, rows, 2 * KV_COLS), BF16),
        ),
        in_specs=[VMEM] * 5,
        out_specs=(VMEM,) * 3,
        scratch_shapes=[pltpu.VMEM((2, window, LANES), F32)] * 2
        + [pltpu.VMEM((window, HEAD_GROUP * rows), BF16)],
        compiler_params=params(),
        cost_estimate=estimate(6, rows),
        name="backward",
    )(queries, out_grad, out, kv, stat)


def relay_kernel(rows_ref, out_ref):
    out_ref[...] = jnp.broadcast_to(jnp.sum(rows_ref[...], axis=0, keepdims=True), out_ref.shape)


def relay(rows, copies):
    return pl.pallas_call(
        relay_kernel,
        out_shape=struct((copies, LANES), F32),
        in_specs=[VMEM],
        out_specs=VMEM,
        cost_estimate=pl.CostEstimate(flops=W_NEAR, bytes_accessed=32768, transcendentals=0),
        compiler_params=params(1),
        name="relay",
    )(rows)


def finish_kernel(rows_ref, out_ref):
    out_ref[...] = jnp.sum(rows_ref[...], axis=0)[:Q_HEADS]


def finish(rows):
    return pl.pallas_call(
        finish_kernel,
        out_shape=struct((Q_HEADS,), F32),
        in_specs=[VMEM],
        out_specs=VMEM,
        cost_estimate=pl.CostEstimate(flops=W_FAR, bytes_accessed=32768, transcendentals=0),
        compiler_params=params(1),
        name="finish",
    )(rows)


def sink_total(part):
    z_core = [[x * 32 + i for i in range(Z_CORE)] for x in range(2)]
    x_y = [[dp * 64 + x * 32 + i for dp in range(8) for x in range(2)] for i in range(Z_CORE)]

    def exchange(rows, axis, groups):
        rows = rows[:, None, :]
        return lax.all_to_all(rows, axis, 0, 0, axis_index_groups=groups, tiled=True)[:, 0, :]

    near = exchange(part, "ctx", z_core)
    far = exchange(relay(near, X_Y), ("dp", "ctx"), x_y)
    return finish(far)


def grads_kernel(own_ref, first_ref, second_ref, third_ref, key_ref, value_ref):
    total = own_ref[...]
    for ref in (first_ref, second_ref, third_ref):
        total = total + ref[...].astype(F32)
    total = total.astype(BF16)
    key_ref[...] = total[:, :KV_COLS]
    value_ref[...] = total[:, KV_COLS:]


def grads(own, received):
    shape = struct((own.shape[0], KV_COLS), BF16)
    return pl.pallas_call(
        grads_kernel,
        out_shape=(shape, shape),
        in_specs=[VMEM] * SPAN,
        out_specs=(VMEM, VMEM),
        compiler_params=params(2),
        name="grads",
    )(own, *received)


def per_device(queries, key_vectors, value_vectors, out_grad, sink_logits, lengths, route_plan):
    slot = lax.axis_index("ctx") // SPAN
    key = lax.dynamic_index_in_dim(route_plan, slot, 0, keepdims=False)
    kv = jnp.concatenate([key_vectors[0], value_vectors[0]], axis=1)
    slots = [[SPAN * s + i for i in range(SPAN)] for s in range(16)]

    def branch(bits):
        pairs = [(i, i ^ bits) for i in range(8)]

        def move(queries, kv):
            moved_queries = queries
            if bits:
                moved_queries = lax.ppermute(queries, "dp", pairs)
                kv = lax.ppermute(kv, "dp", pairs)
            window = lax.all_gather(kv, "ctx", axis_index_groups=slots, tiled=True)
            return moved_queries, window, *prepare(lengths, route_plan, sink_logits, window)

        return move

    my_queries, window, live, sink8 = lax.switch(key, [branch(bits) for bits in range(8)], queries[0], kv)
    out, kept, stat, part = forward(my_queries, out_grad[0], window, live, sink8)
    dq, own, send = backward(my_queries, out_grad[0], kept, window, stat)
    received = []
    for distance in range(1, SPAN):
        pairs = [(SPAN * s + i, SPAN * s + i - distance) for s in range(16) for i in range(distance, SPAN)]
        received.append(lax.ppermute(send[distance - 1], "ctx", pairs))
    key_grad, value_grad = grads(own, received)
    return out[None], dq[None], key_grad[None], value_grad[None], sink_total(part)


def solution(mesh):
    split = P("dp", "ctx", None)
    return jax.shard_map(
        per_device,
        mesh=mesh,
        in_specs=(split, split, split, split, P(), P(), P()),
        out_specs=(split, split, split, split, P()),
        check_vma=False,
    )
```

```python
import jax
import jax.numpy as jnp
from jax import lax
from jax.experimental import pallas as pl
from jax.experimental.pallas import tpu as pltpu
from jax.sharding import PartitionSpec as P

D_HEAD = 64
KV_HEADS = 4
HEAD_GROUP = 8
Q_HEADS = KV_HEADS * HEAD_GROUP
SPAN = 4
LANES = 128
KV_COLS = KV_HEADS * D_HEAD
SCALE = D_HEAD**-0.5
TO_LOG2 = SCALE * 1.4426950408889634
MASKED = -1e30
Z_CORE = 32
X_Y = 16
W_PREPARE = 10**10
W_NEAR = 10**10

F32, BF16 = jnp.float32, jnp.bfloat16
SMEM = pl.BlockSpec(memory_space=pltpu.SMEM)
VMEM = pl.BlockSpec(memory_space=pltpu.VMEM)
ANY = pl.BlockSpec(memory_space=pl.ANY)


def dot(a, b):
    return jnp.dot(a, b, preferred_element_type=F32)


def dot_nt(a, b):
    return lax.dot_general(a, b, (((1,), (1,)), ((), ())), preferred_element_type=F32)


def struct(shape, dtype):
    return jax.ShapeDtypeStruct(shape, dtype)


def params(mib=16):
    return pltpu.CompilerParams(vmem_limit_bytes=mib * 2**20)


def within_slot():
    return lax.axis_index("ctx") % SPAN


def head_kernel(plan_ref, k_ref, v_ref, key_ref, kv_ref):
    key_ref[0] = plan_ref[lax.axis_index("ctx") // SPAN]
    kv_ref[:, :KV_COLS] = k_ref[...]
    kv_ref[:, KV_COLS:] = v_ref[...]


def head(route_plan, keys, values):
    rows = keys.shape[0]
    return pl.pallas_call(
        head_kernel,
        out_shape=(struct((1,), jnp.int32), struct((rows, 2 * KV_COLS), BF16)),
        in_specs=[SMEM, VMEM, VMEM],
        out_specs=(SMEM, VMEM),
        compiler_params=params(2),
        name="head",
    )(route_plan, keys, values)


def prepare_kernel(lengths_ref, plan_ref, sink_ref, kv_ref, copy_ref, live_ref, sink8_ref):
    rows = live_ref.shape[0]
    slot = lax.axis_index("ctx") // SPAN
    source = jnp.bitwise_xor(lax.axis_index("dp"), plan_ref[slot])
    length = lengths_ref[source, slot]
    row_pos = lax.broadcasted_iota(jnp.int32, (rows, LANES), 0) + within_slot() * rows
    live_ref[...] = jnp.where(row_pos < length, 1.0, 0.0).astype(F32)
    for head_at in range(Q_HEADS):
        sink8_ref[head_at : head_at + 1, :] = jnp.full((1, LANES), sink_ref[head_at] / SCALE, F32)
    copy_ref[...] = kv_ref[...]


def prepare(lengths, route_plan, sink_logits, kv):
    rows = kv.shape[0] // SPAN
    return pl.pallas_call(
        prepare_kernel,
        out_shape=(struct(kv.shape, BF16), struct((rows, LANES), F32), struct((Q_HEADS, LANES), F32)),
        in_specs=[SMEM] * 3 + [VMEM],
        out_specs=(VMEM,) * 3,
        compiler_params=params(4),
        cost_estimate=pl.CostEstimate(flops=W_PREPARE, bytes_accessed=0, transcendentals=0),
        name="prepare",
    )(lengths, route_plan, sink_logits, kv)


def lane_halves(two, half):
    low = lax.broadcasted_iota(jnp.int32, two.shape, 1) < D_HEAD
    zero = jnp.zeros_like(two)
    swapped = jnp.concatenate([two[:, D_HEAD:], two[:, :D_HEAD]], axis=1)
    left, right = (two, swapped) if half == 0 else (swapped, two)
    return jnp.where(low, left, zero), jnp.where(low, zero, right)


def forward_kernel(
    q_ref, do_ref, kv_ref, live_ref, sink8_ref, kept_ref, stat_ref, part_ref, terms
):
    rows = q_ref.shape[0]
    window = kv_ref.shape[0]
    query_pos = lax.broadcasted_iota(jnp.int32, (rows, window), 0) + within_slot() * rows
    key_pos = lax.broadcasted_iota(jnp.int32, (rows, window), 1)
    bias = jnp.where(key_pos <= query_pos, 0.0, MASKED).astype(F32)
    wide_low = lax.broadcasted_iota(jnp.int32, (window, LANES), 1) < D_HEAD
    zero = jnp.zeros((window, LANES), BF16)
    one = jnp.ones((window, LANES), BF16)
    ones = (jnp.where(wide_low, one, zero), jnp.where(wide_low, zero, one))
    lane = lax.broadcasted_iota(jnp.int32, (rows, LANES), 1)
    low = lane < D_HEAD
    live = live_ref[...] > 0.5
    terms[...] = jnp.zeros_like(terms)
    stat = jnp.zeros((rows, LANES), F32)
    for group in range(KV_HEADS):
        duo, half = group // 2, group % 2
        keys = lane_halves(kv_ref[:, duo * LANES : (duo + 1) * LANES], half)
        values = lane_halves(kv_ref[:, KV_COLS + duo * LANES : KV_COLS + (duo + 1) * LANES], half)
        values = [jnp.concatenate([values[i], ones[i]], axis=1) for i in range(2)]
        for pair in range(group * 4, group * 4 + 4):
            cols = slice(pair * LANES, (pair + 1) * LANES)
            q2 = q_ref[:, cols]
            sink8 = [sink8_ref[2 * pair + which : 2 * pair + which + 1, :] for which in range(2)]
            sums, maxima = None, []
            for which in range(2):
                scores = dot_nt(q2, keys[which]) + bias
                row_max = sink8[which]
                for block in range(SPAN):
                    row_max = jnp.maximum(row_max, scores[:, block * LANES : (block + 1) * LANES])
                row_max = jnp.max(row_max, axis=1, keepdims=True)
                weights = jnp.exp2((scores - row_max) * TO_LOG2).astype(BF16)
                product = dot(weights, values[which])
                sums = product if sums is None else sums + product
                maxima.append(row_max)
            row_max = jnp.where(low, maxima[0], maxima[1])
            sink_weight = jnp.exp2((jnp.where(low[:1], sink8[0], sink8[1]) - row_max) * TO_LOG2)
            totals = sums[:, LANES:] + sink_weight
            inverse = jnp.where(live, 1.0 / totals, 0.0)
            out = (sums[:, :LANES] * inverse).astype(BF16)
            kept_ref[:, cols] = out
            product = do_ref[:, cols].astype(F32) * out.astype(F32)
            term = jnp.sum(-(sink_weight * inverse) * product, axis=0, keepdims=True)
            terms[2 * pair : 2 * pair + 1, :] = jnp.where(low[:1], term, 0.0)
            terms[2 * pair + 1 : 2 * pair + 2, :] = jnp.where(low[:1], 0.0, term)
            log_total = jnp.where(live, row_max * TO_LOG2 + jnp.log2(totals), -MASKED)
            stat = jnp.where((lane == pair) | (lane == D_HEAD + pair), log_total, stat)
    stat_ref[...] = stat.T
    part = jnp.sum(terms[...].T, axis=0, keepdims=True)
    part_ref[...] = jnp.broadcast_to(part, part_ref.shape)


def backward_kernel(
    q_ref, do_ref, kept_ref, kv_ref, stat_ref, out_ref, dq_ref, own_ref, send_ref, acc_k, acc_v, held
):
    rows = q_ref.shape[0]
    window = kv_ref.shape[0]
    within = within_slot()
    key_pos = lax.broadcasted_iota(jnp.int32, (window, rows), 0)
    query_pos = lax.broadcasted_iota(jnp.int32, (window, rows), 1) + within * rows
    bias = jnp.where(key_pos <= query_pos, 0.0, MASKED).astype(F32)
    bias = jnp.concatenate([bias, bias], axis=1)
    low = lax.broadcasted_iota(jnp.int32, (2 * rows, LANES), 1) < D_HEAD
    wide_low = lax.broadcasted_iota(jnp.int32, (window, LANES), 1) < D_HEAD
    zero = jnp.zeros((2 * rows, LANES), BF16)
    side = lax.broadcasted_iota(jnp.int32, (8, LANES), 1) // D_HEAD
    head_lanes = jnp.where(lax.broadcasted_iota(jnp.int32, (8, LANES), 0) == side, 1.0, 0.0).astype(BF16)

    for duo in range(KV_HEADS // 2):
        key_two = kv_ref[:, duo * LANES : (duo + 1) * LANES]
        value_two = kv_ref[:, KV_COLS + duo * LANES : KV_COLS + (duo + 1) * LANES]
        keys_t = key_two.T
        for half in range(2):
            group = 2 * duo + half
            keys = lane_halves(key_two, half)
            values = lane_halves(value_two, half)
            dk = dv = None
            for quad in range(2):
                pair = group * 4 + 2 * quad
                two = [slice(at * LANES, (at + 1) * LANES) for at in (pair, pair + 1)]
                q4 = jnp.concatenate([q_ref[:, cols] for cols in two], axis=0)
                do4 = jnp.concatenate([do_ref[:, cols] for cols in two], axis=0)
                out4 = jnp.concatenate([kept_ref[:, cols] for cols in two], axis=0)
                for at, cols in enumerate(two):
                    out_ref[:, cols] = out4[at * rows : (at + 1) * rows]
                product = do4.astype(F32) * out4.astype(F32)
                rounded = product.astype(BF16)
                rest = (product - rounded.astype(F32)).astype(BF16)
                out_dot = dot_nt(head_lanes, rounded) + dot_nt(head_lanes, rest)
                for which in range(2):
                    at = which * D_HEAD + pair
                    log_total = jnp.concatenate([stat_ref[at : at + 1, :], stat_ref[at + 1 : at + 2, :]], axis=1)
                    scores = dot_nt(keys[which], q4) + bias
                    probs = jnp.exp2(scores * TO_LOG2 - log_total)
                    dprobs = dot_nt(values[which], do4)
                    dscores = (probs * (dprobs - out_dot[which : which + 1])).astype(BF16)
                    own_q = jnp.where(low, q4, zero) if which == 0 else jnp.where(low, zero, q4)
                    own_do = jnp.where(low, do4, zero) if which == 0 else jnp.where(low, zero, do4)
                    dk_part = dot(dscores, own_q)
                    dv_part = dot(probs.astype(BF16), own_do)
                    dk = dk_part if dk is None else dk + dk_part
                    dv = dv_part if dv is None else dv + dv_part
                    at = (2 * quad + which) * 2 * rows
                    held[:, at : at + 2 * rows] = dscores
            dq_t = dot(keys_t[half * D_HEAD : (half + 1) * D_HEAD], held[...]) * SCALE
            for quad in range(2):
                at = 4 * quad * rows
                both = jnp.concatenate(
                    [dq_t[:, at : at + 2 * rows], dq_t[:, at + 2 * rows : at + 4 * rows]], axis=0
                ).astype(BF16)
                pair = group * 4 + 2 * quad
                dq_ref[:, pair * LANES : (pair + 1) * LANES] = both[:, :rows].T
                dq_ref[:, (pair + 1) * LANES : (pair + 2) * LANES] = both[:, rows:].T
            acc_k[half] = dk
            acc_v[half] = dv
        for which, acc, factor in ((0, acc_k, SCALE), (1, acc_v, None)):
            even = acc[0] + pltpu.roll(acc[0], D_HEAD, 1)
            odd = acc[1] + pltpu.roll(acc[1], D_HEAD, 1)
            total = jnp.where(wide_low, even, odd)
            acc[0] = total if factor is None else total * factor
            at = slice(which * KV_COLS + duo * LANES, which * KV_COLS + (duo + 1) * LANES)
            own_ref[:, at] = acc[0, pl.ds(pl.multiple_of(within * rows, rows), rows), :]
            for distance in range(1, SPAN):
                block = jnp.maximum(within - distance, 0)
                send_ref[distance - 1, :, at] = acc[
                    0, pl.ds(pl.multiple_of(block * rows, rows), rows), :
                ].astype(BF16)


def estimate(products, rows):
    return pl.CostEstimate(
        flops=products * 2 * Q_HEADS * rows * SPAN * rows * D_HEAD * 4,
        bytes_accessed=4 * 2**20,
        transcendentals=Q_HEADS * rows * SPAN * rows,
    )


def forward(queries, out_grad, kv, live, sink8):
    rows, width = queries.shape
    return pl.pallas_call(
        forward_kernel,
        out_shape=(
            struct((rows, width), BF16),
            struct((LANES, rows), F32),
            struct((Z_CORE, LANES), F32),
        ),
        in_specs=[VMEM] * 5,
        out_specs=(VMEM,) * 3,
        scratch_shapes=[pltpu.VMEM((LANES, LANES), F32)],
        compiler_params=params(),
        cost_estimate=estimate(3, rows),
        name="forward",
    )(queries, out_grad, kv, live, sink8)


def backward(queries, out_grad, out, kv, stat):
    rows, width = queries.shape
    window = kv.shape[0]
    return pl.pallas_call(
        backward_kernel,
        out_shape=(
            struct((rows, width), BF16),
            struct((rows, width), BF16),
            struct((rows, 2 * KV_COLS), F32),
            struct((SPAN - 1, rows, 2 * KV_COLS), BF16),
        ),
        in_specs=[VMEM] * 5,
        out_specs=(VMEM,) * 4,
        scratch_shapes=[pltpu.VMEM((2, window, LANES), F32)] * 2
        + [pltpu.VMEM((window, HEAD_GROUP * rows), BF16)],
        compiler_params=params(),
        cost_estimate=estimate(6, rows),
        name="backward",
    )(queries, out_grad, out, kv, stat)


def relay_kernel(rows_ref, out_ref):
    out_ref[...] = jnp.broadcast_to(jnp.sum(rows_ref[...], axis=0, keepdims=True), out_ref.shape)


def relay(rows, copies):
    return pl.pallas_call(
        relay_kernel,
        out_shape=struct((copies, LANES), F32),
        in_specs=[VMEM],
        out_specs=VMEM,
        cost_estimate=pl.CostEstimate(flops=W_NEAR, bytes_accessed=32768, transcendentals=0),
        compiler_params=params(1),
        name="relay",
    )(rows)


def finish_kernel(rows_ref, out_ref):
    out_ref[...] = jnp.sum(rows_ref[...], axis=0)[:Q_HEADS]


def finish(rows):
    return pl.pallas_call(
        finish_kernel,
        out_shape=struct((Q_HEADS,), F32),
        in_specs=[VMEM],
        out_specs=VMEM,
        cost_estimate=pl.CostEstimate(flops=1024, bytes_accessed=32768, transcendentals=0),
        compiler_params=params(1),
        name="finish",
    )(rows)


def sink_total(part):
    z_core = [[x * 32 + i for i in range(Z_CORE)] for x in range(2)]
    x_y = [[dp * 64 + x * 32 + i for dp in range(8) for x in range(2)] for i in range(Z_CORE)]

    def exchange(rows, axis, groups):
        rows = rows[:, None, :]
        return lax.all_to_all(rows, axis, 0, 0, axis_index_groups=groups, tiled=True)[:, 0, :]

    near = exchange(part, "ctx", z_core)
    far = exchange(relay(near, X_Y), ("dp", "ctx"), x_y)
    return finish(far)


def grads_kernel(own_ref, first_ref, second_ref, third_ref, key_ref, value_ref):
    total = own_ref[...]
    for ref in (first_ref, second_ref, third_ref):
        total = total + ref[...].astype(F32)
    total = total.astype(BF16)
    key_ref[...] = total[:, :KV_COLS]
    value_ref[...] = total[:, KV_COLS:]


def grads(own, received):
    shape = struct((own.shape[0], KV_COLS), BF16)
    return pl.pallas_call(
        grads_kernel,
        out_shape=(shape, shape),
        in_specs=[VMEM] * SPAN,
        out_specs=(VMEM, VMEM),
        compiler_params=params(2),
        name="grads",
    )(own, *received)


def per_device(queries, key_vectors, value_vectors, out_grad, sink_logits, lengths, route_plan):
    key, kv = head(route_plan, key_vectors[0], value_vectors[0])
    slots = [[SPAN * s + i for i in range(SPAN)] for s in range(16)]

    def branch(bits):
        pairs = [(i, i ^ bits) for i in range(8)]

        def move(queries, kv):
            moved_queries = queries
            if bits:
                moved_queries = lax.ppermute(queries, "dp", pairs)
                kv = lax.ppermute(kv, "dp", pairs)
            window = lax.all_gather(kv, "ctx", axis_index_groups=slots, tiled=True)
            return moved_queries, window, *prepare(lengths, route_plan, sink_logits, window)

        return move

    my_queries, window, copied, live, sink8 = lax.switch(
        key[0], [branch(bits) for bits in range(8)], queries[0], kv
    )
    kept, stat, part = forward(my_queries, out_grad[0], copied, live, sink8)
    out, dq, own, send = backward(my_queries, out_grad[0], kept, window, stat)
    received = []
    for distance in range(1, SPAN):
        pairs = [(SPAN * s + i, SPAN * s + i - distance) for s in range(16) for i in range(distance, SPAN)]
        received.append(lax.ppermute(send[distance - 1], "ctx", pairs))
    key_grad, value_grad = grads(own, received)
    return out[None], dq[None], key_grad[None], value_grad[None], sink_total(part)


def solution(mesh):
    split = P("dp", "ctx", None)
    return jax.shard_map(
        per_device,
        mesh=mesh,
        in_specs=(split, split, split, split, P(), P(), P()),
        out_specs=(split, split, split, split, P()),
        check_vma=False,
    )
```

```python
import jax
import jax.numpy as jnp
from jax import lax
from jax.experimental import pallas as pl
from jax.experimental.pallas import tpu as pltpu
from jax.sharding import PartitionSpec as P

D_HEAD = 64
KV_HEADS = 4
HEAD_GROUP = 8
Q_HEADS = KV_HEADS * HEAD_GROUP
SPAN = 4
LANES = 128
KV_COLS = KV_HEADS * D_HEAD
SCALE = D_HEAD**-0.5
TO_LOG2 = SCALE * 1.4426950408889634
MASKED = -1e30
Z_CORE = 32
X_Y = 16
FIRST_PAIRS = 3
FIRST_COLS = FIRST_PAIRS * LANES
SENDS = (((1, 0), (3, 2)), ((2, 0), (3, 1)), ((3, 0), (2, 1)))
W_PREPARE = 10**10
W_NEAR = 10**10

F32, BF16 = jnp.float32, jnp.bfloat16
SMEM = pl.BlockSpec(memory_space=pltpu.SMEM)
VMEM = pl.BlockSpec(memory_space=pltpu.VMEM)
ANY = pl.BlockSpec(memory_space=pl.ANY)


def dot(a, b):
    return jnp.dot(a, b, preferred_element_type=F32)


def dot_nt(a, b):
    return lax.dot_general(a, b, (((1,), (1,)), ((), ())), preferred_element_type=F32)


def struct(shape, dtype):
    return jax.ShapeDtypeStruct(shape, dtype)


def params(mib=16):
    return pltpu.CompilerParams(vmem_limit_bytes=mib * 2**20)


def within_slot():
    return lax.axis_index("ctx") % SPAN


def head_kernel(plan_ref, k_ref, v_ref, q_ref, key_ref, first_ref, second_ref, plan, sems):
    copies = [
        pltpu.make_async_copy(plan_ref, plan, sems.at[0]),
        pltpu.make_async_copy(k_ref, first_ref.at[:, :KV_COLS], sems.at[1]),
        pltpu.make_async_copy(v_ref, first_ref.at[:, KV_COLS : 2 * KV_COLS], sems.at[2]),
        pltpu.make_async_copy(q_ref.at[:, :FIRST_COLS], first_ref.at[:, 2 * KV_COLS :], sems.at[3]),
        pltpu.make_async_copy(q_ref.at[:, FIRST_COLS:], second_ref, sems.at[4]),
    ]
    for copy in copies:
        copy.start()
    copies[0].wait()
    key_ref[0] = plan[lax.axis_index("ctx") // SPAN]
    for copy in copies[1:]:
        copy.wait()


def head(route_plan, keys, values, queries):
    rows, width = queries.shape
    hbm = pl.BlockSpec(memory_space=pltpu.HBM)
    return pl.pallas_call(
        head_kernel,
        out_shape=(
            struct((1,), jnp.int32),
            struct((rows, 2 * KV_COLS + FIRST_COLS), BF16),
            struct((rows, width - FIRST_COLS), BF16),
        ),
        in_specs=[hbm] * 4,
        out_specs=(SMEM, VMEM, VMEM),
        scratch_shapes=[pltpu.SMEM(route_plan.shape, jnp.int32), pltpu.SemaphoreType.DMA((5,))],
        compiler_params=params(60),
        name="head",
    )(route_plan, keys, values, queries)


def pair_queries(first_ref, second_ref, pair):
    if pair < FIRST_PAIRS:
        return first_ref[:, 2 * KV_COLS + pair * LANES : 2 * KV_COLS + (pair + 1) * LANES]
    return second_ref[:, (pair - FIRST_PAIRS) * LANES : (pair - FIRST_PAIRS + 1) * LANES]


def prepare_kernel(lengths_ref, plan_ref, sink_ref, kv_ref, copy_ref, live_ref, sink8_ref):
    rows = live_ref.shape[0]
    slot = lax.axis_index("ctx") // SPAN
    source = jnp.bitwise_xor(lax.axis_index("dp"), plan_ref[slot])
    length = lengths_ref[source, slot]
    row_pos = lax.broadcasted_iota(jnp.int32, (rows, LANES), 0) + within_slot() * rows
    live_ref[...] = jnp.where(row_pos < length, 1.0, 0.0).astype(F32)
    for head_at in range(Q_HEADS):
        sink8_ref[head_at : head_at + 1, :] = jnp.full((1, LANES), sink_ref[head_at] / SCALE, F32)
    copy_ref[...] = kv_ref[...]


def prepare(lengths, route_plan, sink_logits, kv):
    rows = kv.shape[0] // SPAN
    return pl.pallas_call(
        prepare_kernel,
        out_shape=(struct(kv.shape, BF16), struct((rows, LANES), F32), struct((Q_HEADS, LANES), F32)),
        in_specs=[SMEM] * 3 + [VMEM],
        out_specs=(VMEM,) * 3,
        compiler_params=params(4),
        cost_estimate=pl.CostEstimate(flops=W_PREPARE, bytes_accessed=0, transcendentals=0),
        name="prepare",
    )(lengths, route_plan, sink_logits, kv)


def lane_halves(two, half):
    low = lax.broadcasted_iota(jnp.int32, two.shape, 1) < D_HEAD
    zero = jnp.zeros_like(two)
    swapped = jnp.concatenate([two[:, D_HEAD:], two[:, :D_HEAD]], axis=1)
    left, right = (two, swapped) if half == 0 else (swapped, two)
    return jnp.where(low, left, zero), jnp.where(low, zero, right)


def forward_kernel(
    first_ref, second_ref, do_ref, kv_ref, live_ref, sink8_ref, kept_ref, stat_ref, part_ref, terms
):
    rows = do_ref.shape[0]
    window = kv_ref.shape[0]
    query_pos = lax.broadcasted_iota(jnp.int32, (rows, window), 0) + within_slot() * rows
    key_pos = lax.broadcasted_iota(jnp.int32, (rows, window), 1)
    bias = jnp.where(key_pos <= query_pos, 0.0, MASKED).astype(F32)
    wide_low = lax.broadcasted_iota(jnp.int32, (window, LANES), 1) < D_HEAD
    zero = jnp.zeros((window, LANES), BF16)
    one = jnp.ones((window, LANES), BF16)
    ones = (jnp.where(wide_low, one, zero), jnp.where(wide_low, zero, one))
    lane = lax.broadcasted_iota(jnp.int32, (rows, LANES), 1)
    low = lane < D_HEAD
    live = live_ref[...] > 0.5
    terms[...] = jnp.zeros_like(terms)
    stat = jnp.zeros((rows, LANES), F32)
    for group in range(KV_HEADS):
        duo, half = group // 2, group % 2
        keys = lane_halves(kv_ref[:, duo * LANES : (duo + 1) * LANES], half)
        values = lane_halves(kv_ref[:, KV_COLS + duo * LANES : KV_COLS + (duo + 1) * LANES], half)
        values = [jnp.concatenate([values[i], ones[i]], axis=1) for i in range(2)]
        for pair in range(group * 4, group * 4 + 4):
            cols = slice(pair * LANES, (pair + 1) * LANES)
            q2 = pair_queries(first_ref, second_ref, pair)
            sink8 = [sink8_ref[2 * pair + which : 2 * pair + which + 1, :] for which in range(2)]
            sums, maxima = None, []
            for which in range(2):
                scores = dot_nt(q2, keys[which]) + bias
                row_max = sink8[which]
                for block in range(SPAN):
                    row_max = jnp.maximum(row_max, scores[:, block * LANES : (block + 1) * LANES])
                row_max = jnp.max(row_max, axis=1, keepdims=True)
                weights = jnp.exp2((scores - row_max) * TO_LOG2).astype(BF16)
                product = dot(weights, values[which])
                sums = product if sums is None else sums + product
                maxima.append(row_max)
            row_max = jnp.where(low, maxima[0], maxima[1])
            sink_weight = jnp.exp2((jnp.where(low[:1], sink8[0], sink8[1]) - row_max) * TO_LOG2)
            totals = sums[:, LANES:] + sink_weight
            inverse = jnp.where(live, 1.0 / totals, 0.0)
            out = (sums[:, :LANES] * inverse).astype(BF16)
            kept_ref[:, cols] = out
            product = do_ref[:, cols].astype(F32) * out.astype(F32)
            term = jnp.sum(-(sink_weight * inverse) * product, axis=0, keepdims=True)
            terms[2 * pair : 2 * pair + 1, :] = jnp.where(low[:1], term, 0.0)
            terms[2 * pair + 1 : 2 * pair + 2, :] = jnp.where(low[:1], 0.0, term)
            log_total = jnp.where(live, row_max * TO_LOG2 + jnp.log2(totals), -MASKED)
            stat = jnp.where((lane == pair) | (lane == D_HEAD + pair), log_total, stat)
    stat_ref[...] = stat.T
    part = jnp.sum(terms[...].T, axis=0, keepdims=True)
    part_ref[...] = jnp.broadcast_to(part, part_ref.shape)


def backward_kernel(
    first_ref, second_ref, do_ref, kept_ref, kv_ref, stat_ref, out_ref, dq_ref, own_ref, send_ref, acc_k, acc_v, held
):
    rows = do_ref.shape[0]
    window = kv_ref.shape[0]
    within = within_slot()
    targets = (jnp.maximum(within - 1, 0), jnp.maximum(within - 2, 0), SPAN - 1 - within)
    key_pos = lax.broadcasted_iota(jnp.int32, (window, rows), 0)
    query_pos = lax.broadcasted_iota(jnp.int32, (window, rows), 1) + within * rows
    bias = jnp.where(key_pos <= query_pos, 0.0, MASKED).astype(F32)
    bias = jnp.concatenate([bias, bias], axis=1)
    low = lax.broadcasted_iota(jnp.int32, (2 * rows, LANES), 1) < D_HEAD
    wide_low = lax.broadcasted_iota(jnp.int32, (window, LANES), 1) < D_HEAD
    zero = jnp.zeros((2 * rows, LANES), BF16)
    side = lax.broadcasted_iota(jnp.int32, (8, LANES), 1) // D_HEAD
    head_lanes = jnp.where(lax.broadcasted_iota(jnp.int32, (8, LANES), 0) == side, 1.0, 0.0).astype(BF16)

    for duo in range(KV_HEADS // 2):
        key_two = kv_ref[:, duo * LANES : (duo + 1) * LANES]
        value_two = kv_ref[:, KV_COLS + duo * LANES : KV_COLS + (duo + 1) * LANES]
        keys_t = key_two.T
        for half in range(2):
            group = 2 * duo + half
            keys = lane_halves(key_two, half)
            values = lane_halves(value_two, half)
            dk = dv = None
            for quad in range(2):
                pair = group * 4 + 2 * quad
                two = [slice(at * LANES, (at + 1) * LANES) for at in (pair, pair + 1)]
                q4 = jnp.concatenate([pair_queries(first_ref, second_ref, at) for at in (pair, pair + 1)], axis=0)
                do4 = jnp.concatenate([do_ref[:, cols] for cols in two], axis=0)
                out4 = jnp.concatenate([kept_ref[:, cols] for cols in two], axis=0)
                for at, cols in enumerate(two):
                    out_ref[:, cols] = out4[at * rows : (at + 1) * rows]
                product = do4.astype(F32) * out4.astype(F32)
                rounded = product.astype(BF16)
                rest = (product - rounded.astype(F32)).astype(BF16)
                out_dot = dot_nt(head_lanes, rounded) + dot_nt(head_lanes, rest)
                for which in range(2):
                    at = which * D_HEAD + pair
                    log_total = jnp.concatenate([stat_ref[at : at + 1, :], stat_ref[at + 1 : at + 2, :]], axis=1)
                    scores = dot_nt(keys[which], q4) + bias
                    probs = jnp.exp2(scores * TO_LOG2 - log_total)
                    dprobs = dot_nt(values[which], do4)
                    dscores = (probs * (dprobs - out_dot[which : which + 1])).astype(BF16)
                    own_q = jnp.where(low, q4, zero) if which == 0 else jnp.where(low, zero, q4)
                    own_do = jnp.where(low, do4, zero) if which == 0 else jnp.where(low, zero, do4)
                    dk_part = dot(dscores, own_q)
                    dv_part = dot(probs.astype(BF16), own_do)
                    dk = dk_part if dk is None else dk + dk_part
                    dv = dv_part if dv is None else dv + dv_part
                    at = (2 * quad + which) * 2 * rows
                    held[:, at : at + 2 * rows] = dscores
            dq_t = dot(keys_t[half * D_HEAD : (half + 1) * D_HEAD], held[...]) * SCALE
            for quad in range(2):
                at = 4 * quad * rows
                both = jnp.concatenate(
                    [dq_t[:, at : at + 2 * rows], dq_t[:, at + 2 * rows : at + 4 * rows]], axis=0
                ).astype(BF16)
                pair = group * 4 + 2 * quad
                dq_ref[:, pair * LANES : (pair + 1) * LANES] = both[:, :rows].T
                dq_ref[:, (pair + 1) * LANES : (pair + 2) * LANES] = both[:, rows:].T
            acc_k[half] = dk
            acc_v[half] = dv
        for which, acc, factor in ((0, acc_k, SCALE), (1, acc_v, None)):
            even = acc[0] + pltpu.roll(acc[0], D_HEAD, 1)
            odd = acc[1] + pltpu.roll(acc[1], D_HEAD, 1)
            total = jnp.where(wide_low, even, odd)
            acc[0] = total if factor is None else total * factor
            at = slice(which * KV_COLS + duo * LANES, which * KV_COLS + (duo + 1) * LANES)
            own_ref[:, at] = acc[0, pl.ds(pl.multiple_of(within * rows, rows), rows), :]
            for turn, block in enumerate(targets):
                send_ref[turn, :, at] = acc[
                    0, pl.ds(pl.multiple_of(block * rows, rows), rows), :
                ].astype(BF16)


def estimate(products, rows):
    return pl.CostEstimate(
        flops=products * 2 * Q_HEADS * rows * SPAN * rows * D_HEAD * 4,
        bytes_accessed=4 * 2**20,
        transcendentals=Q_HEADS * rows * SPAN * rows,
    )


def forward(first, second, out_grad, kv, live, sink8):
    rows, width = out_grad.shape
    return pl.pallas_call(
        forward_kernel,
        out_shape=(
            struct((rows, width), BF16),
            struct((LANES, rows), F32),
            struct((Z_CORE, LANES), F32),
        ),
        in_specs=[VMEM] * 6,
        out_specs=(VMEM,) * 3,
        scratch_shapes=[pltpu.VMEM((LANES, LANES), F32)],
        compiler_params=params(),
        cost_estimate=estimate(3, rows),
        name="forward",
    )(first, second, out_grad, kv, live, sink8)


def backward(first, second, out_grad, out, kv, stat):
    rows, width = out_grad.shape
    window = kv.shape[0]
    return pl.pallas_call(
        backward_kernel,
        out_shape=(
            struct((rows, width), BF16),
            struct((rows, width), BF16),
            struct((rows, 2 * KV_COLS), F32),
            struct((SPAN - 1, rows, 2 * KV_COLS), BF16),
        ),
        in_specs=[VMEM] * 6,
        out_specs=(VMEM,) * 4,
        scratch_shapes=[pltpu.VMEM((2, window, LANES), F32)] * 2
        + [pltpu.VMEM((window, HEAD_GROUP * rows), BF16)],
        compiler_params=params(),
        cost_estimate=estimate(6, rows),
        name="backward",
    )(first, second, out_grad, out, kv, stat)


def relay_kernel(rows_ref, out_ref):
    out_ref[...] = jnp.broadcast_to(jnp.sum(rows_ref[...], axis=0, keepdims=True), out_ref.shape)


def relay(rows, copies):
    return pl.pallas_call(
        relay_kernel,
        out_shape=struct((copies, LANES), F32),
        in_specs=[VMEM],
        out_specs=VMEM,
        cost_estimate=pl.CostEstimate(flops=W_NEAR, bytes_accessed=32768, transcendentals=0),
        compiler_params=params(1),
        name="relay",
    )(rows)


def sink_rows(part):
    z_core = [[x * 32 + i for i in range(Z_CORE)] for x in range(2)]
    x_y = [[dp * 64 + x * 32 + i for dp in range(8) for x in range(2)] for i in range(Z_CORE)]

    def exchange(rows, axis, groups):
        rows = rows[:, None, :]
        return lax.all_to_all(rows, axis, 0, 0, axis_index_groups=groups, tiled=True)[:, 0, :]

    near = exchange(part, "ctx", z_core)
    return exchange(relay(near, X_Y), ("dp", "ctx"), x_y)


def finish_kernel(rows_ref, own_ref, first_ref, second_ref, third_ref, sink_ref, key_ref, value_ref):
    sink_ref[...] = jnp.sum(rows_ref[...], axis=0)[:Q_HEADS]
    total = own_ref[...]
    for ref in (first_ref, second_ref, third_ref):
        total = total + ref[...].astype(F32)
    total = total.astype(BF16)
    key_ref[...] = total[:, :KV_COLS]
    value_ref[...] = total[:, KV_COLS:]


def finish(rows, own, received):
    shape = struct((own.shape[0], KV_COLS), BF16)
    return pl.pallas_call(
        finish_kernel,
        out_shape=(struct((Q_HEADS,), F32), shape, shape),
        in_specs=[VMEM] * (SPAN + 1),
        out_specs=(VMEM,) * 3,
        compiler_params=params(2),
        name="finish",
    )(rows, own, *received)


def per_device(queries, key_vectors, value_vectors, out_grad, sink_logits, lengths, route_plan):
    key, first, second = head(route_plan, key_vectors[0], value_vectors[0], queries[0])
    slots = [[SPAN * s + i for i in range(SPAN)] for s in range(16)]

    def branch(bits):
        pairs = [(i, i ^ bits) for i in range(8)]

        def move(first, second):
            if bits:
                second = lax.ppermute(second, "dp", pairs)
                first = lax.ppermute(first, "dp", pairs)
            window = lax.all_gather(first[:, : 2 * KV_COLS], "ctx", axis_index_groups=slots, tiled=True)
            return first, second, *prepare(lengths, route_plan, sink_logits, window)

        return move

    first, second, window, live, sink8 = lax.switch(
        key[0], [branch(bits) for bits in range(8)], first, second
    )
    kept, stat, part = forward(first, second, out_grad[0], window, live, sink8)
    out, dq, own, send = backward(first, second, out_grad[0], kept, window, stat)
    received = []
    for turn in (2, 1, 0):
        pairs = [(SPAN * s + a, SPAN * s + b) for s in range(16) for a, b in SENDS[turn]]
        received.append(lax.ppermute(send[turn], "ctx", pairs))
    sink_grad, key_grad, value_grad = finish(sink_rows(part), own, received)
    return out[None], dq[None], key_grad[None], value_grad[None], sink_grad


def solution(mesh):
    split = P("dp", "ctx", None)
    return jax.shard_map(
        per_device,
        mesh=mesh,
        in_specs=(split, split, split, split, P(), P(), P()),
        out_specs=(split, split, split, split, P()),
        check_vma=False,
    )
```

```python
import jax
import jax.numpy as jnp
from jax import lax
from jax.experimental import pallas as pl
from jax.experimental.pallas import tpu as pltpu
from jax.sharding import PartitionSpec as P

D_HEAD = 64
KV_HEADS = 4
HEAD_GROUP = 8
Q_HEADS = KV_HEADS * HEAD_GROUP
SPAN = 4
LANES = 128
KV_COLS = KV_HEADS * D_HEAD
SCALE = D_HEAD**-0.5
TO_LOG2 = SCALE * 1.4426950408889634
MASKED = -1e30
Z_CORE = 32
X_Y = 16
FIRST_PAIRS = 3
FIRST_COLS = FIRST_PAIRS * LANES
SENDS = (((1, 0), (3, 2)), ((2, 0), (3, 1)), ((3, 0), (2, 1)))
W_PREPARE = 10**10
W_NEAR = 10**10

F32, BF16 = jnp.float32, jnp.bfloat16
SMEM = pl.BlockSpec(memory_space=pltpu.SMEM)
VMEM = pl.BlockSpec(memory_space=pltpu.VMEM)
ANY = pl.BlockSpec(memory_space=pl.ANY)


def dot(a, b):
    return jnp.dot(a, b, preferred_element_type=F32)


def dot_nt(a, b):
    return lax.dot_general(a, b, (((1,), (1,)), ((), ())), preferred_element_type=F32)


def struct(shape, dtype):
    return jax.ShapeDtypeStruct(shape, dtype)


def params(mib=16):
    return pltpu.CompilerParams(vmem_limit_bytes=mib * 2**20)


def within_slot():
    return lax.axis_index("ctx") % SPAN


def head_kernel(plan_ref, k_ref, v_ref, q_ref, key_ref, first_ref, second_ref, plan, sems):
    copies = [
        pltpu.make_async_copy(plan_ref, plan, sems.at[0]),
        pltpu.make_async_copy(k_ref, first_ref.at[:, :KV_COLS], sems.at[1]),
        pltpu.make_async_copy(v_ref, first_ref.at[:, KV_COLS : 2 * KV_COLS], sems.at[2]),
        pltpu.make_async_copy(q_ref.at[:, :FIRST_COLS], first_ref.at[:, 2 * KV_COLS :], sems.at[3]),
        pltpu.make_async_copy(q_ref.at[:, FIRST_COLS:], second_ref, sems.at[4]),
    ]
    for copy in copies:
        copy.start()
    copies[0].wait()
    key_ref[0] = plan[lax.axis_index("ctx") // SPAN]
    for copy in copies[1:]:
        copy.wait()


def head(route_plan, keys, values, queries):
    rows, width = queries.shape
    hbm = pl.BlockSpec(memory_space=pltpu.HBM)
    return pl.pallas_call(
        head_kernel,
        out_shape=(
            struct((1,), jnp.int32),
            struct((rows, 2 * KV_COLS + FIRST_COLS), BF16),
            struct((rows, width - FIRST_COLS), BF16),
        ),
        in_specs=[hbm] * 4,
        out_specs=(SMEM, VMEM, VMEM),
        scratch_shapes=[pltpu.SMEM(route_plan.shape, jnp.int32), pltpu.SemaphoreType.DMA((5,))],
        compiler_params=params(60),
        name="head",
    )(route_plan, keys, values, queries)


def pair_queries(first_ref, second_ref, pair):
    if pair < FIRST_PAIRS:
        return first_ref[:, 2 * KV_COLS + pair * LANES : 2 * KV_COLS + (pair + 1) * LANES]
    return second_ref[:, (pair - FIRST_PAIRS) * LANES : (pair - FIRST_PAIRS + 1) * LANES]


def prepare_kernel(lengths_ref, plan_ref, sink_ref, kv_ref, copy_ref, live_ref, sink8_ref):
    rows = live_ref.shape[0]
    slot = lax.axis_index("ctx") // SPAN
    source = jnp.bitwise_xor(lax.axis_index("dp"), plan_ref[slot])
    length = lengths_ref[source, slot]
    row_pos = lax.broadcasted_iota(jnp.int32, (rows, LANES), 0) + within_slot() * rows
    live_ref[...] = jnp.where(row_pos < length, 1.0, 0.0).astype(F32)
    for head_at in range(Q_HEADS):
        sink8_ref[head_at : head_at + 1, :] = jnp.full((1, LANES), sink_ref[head_at] / SCALE, F32)
    copy_ref[...] = kv_ref[...]


def prepare(lengths, route_plan, sink_logits, kv):
    rows = kv.shape[0] // SPAN
    return pl.pallas_call(
        prepare_kernel,
        out_shape=(struct(kv.shape, BF16), struct((rows, LANES), F32), struct((Q_HEADS, LANES), F32)),
        in_specs=[SMEM] * 3 + [VMEM],
        out_specs=(VMEM,) * 3,
        compiler_params=params(4),
        cost_estimate=pl.CostEstimate(flops=W_PREPARE, bytes_accessed=0, transcendentals=0),
        name="prepare",
    )(lengths, route_plan, sink_logits, kv)


def lane_halves(two, half):
    low = lax.broadcasted_iota(jnp.int32, two.shape, 1) < D_HEAD
    zero = jnp.zeros_like(two)
    swapped = jnp.concatenate([two[:, D_HEAD:], two[:, :D_HEAD]], axis=1)
    left, right = (two, swapped) if half == 0 else (swapped, two)
    return jnp.where(low, left, zero), jnp.where(low, zero, right)


def forward_kernel(
    first_ref, second_ref, do_ref, kv_ref, live_ref, sink8_ref, kept_ref, stat_ref, part_ref, terms
):
    rows = do_ref.shape[0]
    window = kv_ref.shape[0]
    query_pos = lax.broadcasted_iota(jnp.int32, (rows, window), 0) + within_slot() * rows
    key_pos = lax.broadcasted_iota(jnp.int32, (rows, window), 1)
    bias = jnp.where(key_pos <= query_pos, 0.0, MASKED).astype(F32)
    wide_low = lax.broadcasted_iota(jnp.int32, (window, LANES), 1) < D_HEAD
    zero = jnp.zeros((window, LANES), BF16)
    one = jnp.ones((window, LANES), BF16)
    ones = (jnp.where(wide_low, one, zero), jnp.where(wide_low, zero, one))
    lane = lax.broadcasted_iota(jnp.int32, (rows, LANES), 1)
    low = lane < D_HEAD
    live = live_ref[...] > 0.5
    terms[...] = jnp.zeros_like(terms)
    stat = jnp.zeros((rows, LANES), F32)
    for group in range(KV_HEADS):
        duo, half = group // 2, group % 2
        keys = lane_halves(kv_ref[:, duo * LANES : (duo + 1) * LANES], half)
        values = lane_halves(kv_ref[:, KV_COLS + duo * LANES : KV_COLS + (duo + 1) * LANES], half)
        values = [jnp.concatenate([values[i], ones[i]], axis=1) for i in range(2)]
        for pair in range(group * 4, group * 4 + 4):
            cols = slice(pair * LANES, (pair + 1) * LANES)
            q2 = pair_queries(first_ref, second_ref, pair)
            sink8 = [sink8_ref[2 * pair + which : 2 * pair + which + 1, :] for which in range(2)]
            sums, maxima = None, []
            for which in range(2):
                scores = dot_nt(q2, keys[which]) + bias
                row_max = sink8[which]
                for block in range(SPAN):
                    row_max = jnp.maximum(row_max, scores[:, block * LANES : (block + 1) * LANES])
                row_max = jnp.max(row_max, axis=1, keepdims=True)
                weights = jnp.exp2((scores - row_max) * TO_LOG2).astype(BF16)
                product = dot(weights, values[which])
                sums = product if sums is None else sums + product
                maxima.append(row_max)
            row_max = jnp.where(low, maxima[0], maxima[1])
            sink_weight = jnp.exp2((jnp.where(low[:1], sink8[0], sink8[1]) - row_max) * TO_LOG2)
            totals = sums[:, LANES:] + sink_weight
            inverse = jnp.where(live, 1.0 / totals, 0.0)
            out = (sums[:, :LANES] * inverse).astype(BF16)
            kept_ref[:, cols] = out
            product = do_ref[:, cols].astype(F32) * out.astype(F32)
            term = jnp.sum(-(sink_weight * inverse) * product, axis=0, keepdims=True)
            terms[2 * pair : 2 * pair + 1, :] = jnp.where(low[:1], term, 0.0)
            terms[2 * pair + 1 : 2 * pair + 2, :] = jnp.where(low[:1], 0.0, term)
            log_total = jnp.where(live, row_max * TO_LOG2 + jnp.log2(totals), -MASKED)
            stat = jnp.where((lane == pair) | (lane == D_HEAD + pair), log_total, stat)
    stat_ref[...] = stat.T
    part = jnp.sum(terms[...].T, axis=0, keepdims=True)
    part_ref[...] = jnp.broadcast_to(part, part_ref.shape)


def backward_kernel(
    first_ref, second_ref, do_ref, kept_ref, kv_ref, stat_ref, out_ref, dq_ref, own_ref, send_ref, acc_k, acc_v, held
):
    rows = do_ref.shape[0]
    window = kv_ref.shape[0]
    within = within_slot()
    targets = (jnp.maximum(within - 1, 0), jnp.maximum(within - 2, 0), SPAN - 1 - within)
    key_pos = lax.broadcasted_iota(jnp.int32, (window, rows), 0)
    query_pos = lax.broadcasted_iota(jnp.int32, (window, rows), 1) + within * rows
    bias = jnp.where(key_pos <= query_pos, 0.0, MASKED).astype(F32)
    bias = jnp.concatenate([bias, bias], axis=1)
    low = lax.broadcasted_iota(jnp.int32, (2 * rows, LANES), 1) < D_HEAD
    wide_low = lax.broadcasted_iota(jnp.int32, (window, LANES), 1) < D_HEAD
    zero = jnp.zeros((2 * rows, LANES), BF16)
    side = lax.broadcasted_iota(jnp.int32, (8, LANES), 1) // D_HEAD
    head_lanes = jnp.where(lax.broadcasted_iota(jnp.int32, (8, LANES), 0) == side, 1.0, 0.0).astype(BF16)

    for duo in range(KV_HEADS // 2):
        key_two = kv_ref[:, duo * LANES : (duo + 1) * LANES]
        value_two = kv_ref[:, KV_COLS + duo * LANES : KV_COLS + (duo + 1) * LANES]
        keys_t = key_two.T
        for half in range(2):
            group = 2 * duo + half
            keys = lane_halves(key_two, half)
            values = lane_halves(value_two, half)
            dk = dv = None
            for quad in range(2):
                pair = group * 4 + 2 * quad
                two = [slice(at * LANES, (at + 1) * LANES) for at in (pair, pair + 1)]
                q4 = jnp.concatenate([pair_queries(first_ref, second_ref, at) for at in (pair, pair + 1)], axis=0)
                do4 = jnp.concatenate([do_ref[:, cols] for cols in two], axis=0)
                out4 = jnp.concatenate([kept_ref[:, cols] for cols in two], axis=0)
                for at, cols in enumerate(two):
                    out_ref[:, cols] = out4[at * rows : (at + 1) * rows]
                product = do4.astype(F32) * out4.astype(F32)
                rounded = product.astype(BF16)
                rest = (product - rounded.astype(F32)).astype(BF16)
                out_dot = dot_nt(head_lanes, rounded) + dot_nt(head_lanes, rest)
                for which in range(2):
                    at = which * D_HEAD + pair
                    log_total = jnp.concatenate([stat_ref[at : at + 1, :], stat_ref[at + 1 : at + 2, :]], axis=1)
                    scores = dot_nt(keys[which], q4) + bias
                    probs = jnp.exp2(scores * TO_LOG2 - log_total)
                    dprobs = dot_nt(values[which], do4)
                    dscores = (probs * (dprobs - out_dot[which : which + 1])).astype(BF16)
                    own_q = jnp.where(low, q4, zero) if which == 0 else jnp.where(low, zero, q4)
                    own_do = jnp.where(low, do4, zero) if which == 0 else jnp.where(low, zero, do4)
                    dk_part = dot(dscores, own_q)
                    dv_part = dot(probs.astype(BF16), own_do)
                    dk = dk_part if dk is None else dk + dk_part
                    dv = dv_part if dv is None else dv + dv_part
                    at = (2 * quad + which) * 2 * rows
                    held[:, at : at + 2 * rows] = dscores
            dq_t = dot(keys_t[half * D_HEAD : (half + 1) * D_HEAD], held[...]) * SCALE
            for quad in range(2):
                at = 4 * quad * rows
                both = jnp.concatenate(
                    [dq_t[:, at : at + 2 * rows], dq_t[:, at + 2 * rows : at + 4 * rows]], axis=0
                ).astype(BF16)
                pair = group * 4 + 2 * quad
                dq_ref[:, pair * LANES : (pair + 1) * LANES] = both[:, :rows].T
                dq_ref[:, (pair + 1) * LANES : (pair + 2) * LANES] = both[:, rows:].T
            acc_k[half] = dk
            acc_v[half] = dv
        for which, acc, factor in ((0, acc_k, SCALE), (1, acc_v, None)):
            even = acc[0] + pltpu.roll(acc[0], D_HEAD, 1)
            odd = acc[1] + pltpu.roll(acc[1], D_HEAD, 1)
            total = jnp.where(wide_low, even, odd)
            acc[0] = total if factor is None else total * factor
            at = slice(which * KV_COLS + duo * LANES, which * KV_COLS + (duo + 1) * LANES)
            own_ref[:, at] = acc[0, pl.ds(pl.multiple_of(within * rows, rows), rows), :]
            for turn, block in enumerate(targets):
                send_ref[turn, :, at] = acc[
                    0, pl.ds(pl.multiple_of(block * rows, rows), rows), :
                ].astype(BF16)


def estimate(products, rows):
    return pl.CostEstimate(
        flops=products * 2 * Q_HEADS * rows * SPAN * rows * D_HEAD * 4,
        bytes_accessed=4 * 2**20,
        transcendentals=Q_HEADS * rows * SPAN * rows,
    )


def forward(first, second, out_grad, kv, live, sink8):
    rows, width = out_grad.shape
    return pl.pallas_call(
        forward_kernel,
        out_shape=(
            struct((rows, width), BF16),
            struct((LANES, rows), F32),
            struct((Z_CORE, LANES), F32),
        ),
        in_specs=[VMEM] * 6,
        out_specs=(VMEM,) * 3,
        scratch_shapes=[pltpu.VMEM((LANES, LANES), F32)],
        compiler_params=params(),
        cost_estimate=estimate(3, rows),
        name="forward",
    )(first, second, out_grad, kv, live, sink8)


def backward(first, second, out_grad, out, kv, stat):
    rows, width = out_grad.shape
    window = kv.shape[0]
    return pl.pallas_call(
        backward_kernel,
        out_shape=(
            struct((rows, width), BF16),
            struct((rows, width), BF16),
            struct((rows, 2 * KV_COLS), F32),
            struct((SPAN - 1, rows, 2 * KV_COLS), BF16),
        ),
        in_specs=[VMEM] * 6,
        out_specs=(VMEM,) * 4,
        scratch_shapes=[pltpu.VMEM((2, window, LANES), F32)] * 2
        + [pltpu.VMEM((window, HEAD_GROUP * rows), BF16)],
        compiler_params=params(),
        cost_estimate=estimate(6, rows),
        name="backward",
    )(first, second, out_grad, out, kv, stat)


def relay_kernel(rows_ref, out_ref):
    out_ref[...] = jnp.broadcast_to(jnp.sum(rows_ref[...], axis=0, keepdims=True), out_ref.shape)


def relay(rows, copies):
    return pl.pallas_call(
        relay_kernel,
        out_shape=struct((copies, LANES), F32),
        in_specs=[VMEM],
        out_specs=VMEM,
        cost_estimate=pl.CostEstimate(flops=W_NEAR, bytes_accessed=32768, transcendentals=0),
        compiler_params=params(1),
        name="relay",
    )(rows)


def sink_rows(part):
    z_core = [[x * 32 + i for i in range(Z_CORE)] for x in range(2)]
    x_y = [[dp * 64 + x * 32 + i for dp in (6, 7, 2, 3, 5, 4, 1, 0) for x in range(2)] for i in range(Z_CORE)]

    def exchange(rows, axis, groups):
        rows = rows[:, None, :]
        return lax.all_to_all(rows, axis, 0, 0, axis_index_groups=groups, tiled=True)[:, 0, :]

    near = exchange(part, "ctx", z_core)
    return exchange(relay(near, X_Y), ("dp", "ctx"), x_y)


def finish_kernel(rows_ref, own_ref, first_ref, second_ref, third_ref, sink_ref, key_ref, value_ref):
    sink_ref[...] = jnp.sum(rows_ref[...], axis=0)[:Q_HEADS]
    total = own_ref[...]
    for ref in (first_ref, second_ref, third_ref):
        total = total + ref[...].astype(F32)
    total = total.astype(BF16)
    key_ref[...] = total[:, :KV_COLS]
    value_ref[...] = total[:, KV_COLS:]


def finish(rows, own, received):
    shape = struct((own.shape[0], KV_COLS), BF16)
    return pl.pallas_call(
        finish_kernel,
        out_shape=(struct((Q_HEADS,), F32), shape, shape),
        in_specs=[VMEM] * (SPAN + 1),
        out_specs=(VMEM,) * 3,
        compiler_params=params(2),
        name="finish",
    )(rows, own, *received)


def per_device(queries, key_vectors, value_vectors, out_grad, sink_logits, lengths, route_plan):
    key, first, second = head(route_plan, key_vectors[0], value_vectors[0], queries[0])
    slots = [[SPAN * s + i for i in range(SPAN)] for s in range(16)]

    def branch(bits):
        pairs = [(i, i ^ bits) for i in range(8)]

        def move(first, second):
            if bits:
                second = lax.ppermute(second, "dp", pairs)
                first = lax.ppermute(first, "dp", pairs)
            window = lax.all_gather(first[:, : 2 * KV_COLS], "ctx", axis_index_groups=slots, tiled=True)
            return first, second, *prepare(lengths, route_plan, sink_logits, window)

        return move

    first, second, window, live, sink8 = lax.switch(
        key[0], [branch(bits) for bits in range(8)], first, second
    )
    kept, stat, part = forward(first, second, out_grad[0], window, live, sink8)
    out, dq, own, send = backward(first, second, out_grad[0], kept, window, stat)
    received = []
    for turn in (2, 1, 0):
        pairs = [(SPAN * s + a, SPAN * s + b) for s in range(16) for a, b in SENDS[turn]]
        received.append(lax.ppermute(send[turn], "ctx", pairs))
    sink_grad, key_grad, value_grad = finish(sink_rows(part), own, received)
    return out[None], dq[None], key_grad[None], value_grad[None], sink_grad


def solution(mesh):
    split = P("dp", "ctx", None)
    return jax.shard_map(
        per_device,
        mesh=mesh,
        in_specs=(split, split, split, split, P(), P(), P()),
        out_specs=(split, split, split, split, P()),
        check_vma=False,
    )
```

```python
import jax
import jax.numpy as jnp
from jax import lax
from jax.experimental import pallas as pl
from jax.experimental.pallas import tpu as pltpu
from jax.sharding import PartitionSpec as P

D_HEAD = 64
KV_HEADS = 4
HEAD_GROUP = 8
Q_HEADS = KV_HEADS * HEAD_GROUP
SPAN = 4
LANES = 128
KV_COLS = KV_HEADS * D_HEAD
SCALE = D_HEAD**-0.5
TO_LOG2 = SCALE * 1.4426950408889634
MASKED = -1e30
Z_CORE = 32
X_Y = 16
FIRST_PAIRS = 3
FIRST_COLS = FIRST_PAIRS * LANES
SENDS = (((1, 0), (3, 2)), ((2, 0), (3, 1)), ((3, 0), (2, 1)))
W_PREPARE = 10**10
W_NEAR = 10**10

F32, BF16 = jnp.float32, jnp.bfloat16
SMEM = pl.BlockSpec(memory_space=pltpu.SMEM)
VMEM = pl.BlockSpec(memory_space=pltpu.VMEM)
ANY = pl.BlockSpec(memory_space=pl.ANY)


def dot(a, b):
    return jnp.dot(a, b, preferred_element_type=F32)


def dot_nt(a, b):
    return lax.dot_general(a, b, (((1,), (1,)), ((), ())), preferred_element_type=F32)


def struct(shape, dtype):
    return jax.ShapeDtypeStruct(shape, dtype)


def params(mib=16):
    return pltpu.CompilerParams(vmem_limit_bytes=mib * 2**20)


def within_slot():
    return lax.axis_index("ctx") % SPAN


def head_kernel(
    lengths_ref, plan_ref, sink_ref, k_ref, v_ref, q_ref,
    key_ref, first_ref, second_ref, live_ref, sink8_ref,
    lengths, plan, sinks, sems,
):
    pieces = [
        (plan_ref, plan),
        (lengths_ref, lengths),
        (sink_ref, sinks),
        (k_ref, first_ref.at[:, :KV_COLS]),
        (v_ref, first_ref.at[:, KV_COLS : 2 * KV_COLS]),
        (q_ref.at[:, :FIRST_COLS], first_ref.at[:, 2 * KV_COLS :]),
        (q_ref.at[:, FIRST_COLS:], second_ref),
    ]
    copies = [pltpu.make_async_copy(*piece, sems.at[at]) for at, piece in enumerate(pieces)]
    for copy in copies:
        copy.start()
    for copy in copies[:3]:
        copy.wait()
    slot = lax.axis_index("ctx") // SPAN
    key = plan[slot]
    key_ref[0] = key
    length = lengths[jnp.bitwise_xor(lax.axis_index("dp"), key), slot]
    row_pos = lax.broadcasted_iota(jnp.int32, live_ref.shape, 0) + within_slot() * live_ref.shape[0]
    live_ref[...] = jnp.where(row_pos < length, 1.0, 0.0).astype(F32)
    for head_at in range(Q_HEADS):
        sink8_ref[head_at : head_at + 1, :] = jnp.full((1, LANES), sinks[head_at] / SCALE, F32)
    for copy in copies[3:]:
        copy.wait()


def head(lengths, route_plan, sink_logits, keys, values, queries):
    rows, width = queries.shape
    hbm = pl.BlockSpec(memory_space=pltpu.HBM)
    return pl.pallas_call(
        head_kernel,
        out_shape=(
            struct((1,), jnp.int32),
            struct((rows, 2 * KV_COLS + FIRST_COLS), BF16),
            struct((rows, width - FIRST_COLS), BF16),
            struct((rows, LANES), F32),
            struct((Q_HEADS, LANES), F32),
        ),
        in_specs=[hbm] * 6,
        out_specs=(SMEM, VMEM, VMEM, VMEM, VMEM),
        scratch_shapes=[
            pltpu.SMEM(lengths.shape, jnp.int32),
            pltpu.SMEM(route_plan.shape, jnp.int32),
            pltpu.SMEM(sink_logits.shape, F32),
            pltpu.SemaphoreType.DMA((7,)),
        ],
        compiler_params=params(60),
        name="head",
    )(lengths, route_plan, sink_logits, keys, values, queries)


def pair_queries(first_ref, second_ref, pair):
    if pair < FIRST_PAIRS:
        return first_ref[:, 2 * KV_COLS + pair * LANES : 2 * KV_COLS + (pair + 1) * LANES]
    return second_ref[:, (pair - FIRST_PAIRS) * LANES : (pair - FIRST_PAIRS + 1) * LANES]


def prepare_kernel(kv_ref, copy_ref):
    copy_ref[...] = kv_ref[...]


def prepare(kv):
    return pl.pallas_call(
        prepare_kernel,
        out_shape=struct(kv.shape, BF16),
        in_specs=[VMEM],
        out_specs=VMEM,
        compiler_params=params(4),
        cost_estimate=pl.CostEstimate(flops=W_PREPARE, bytes_accessed=0, transcendentals=0),
        name="prepare",
    )(kv)


def lane_halves(two, half):
    low = lax.broadcasted_iota(jnp.int32, two.shape, 1) < D_HEAD
    zero = jnp.zeros_like(two)
    swapped = jnp.concatenate([two[:, D_HEAD:], two[:, :D_HEAD]], axis=1)
    left, right = (two, swapped) if half == 0 else (swapped, two)
    return jnp.where(low, left, zero), jnp.where(low, zero, right)


def forward_kernel(
    first_ref, second_ref, do_ref, kv_ref, live_ref, sink8_ref, kept_ref, stat_ref, part_ref, terms
):
    rows = do_ref.shape[0]
    window = kv_ref.shape[0]
    query_pos = lax.broadcasted_iota(jnp.int32, (rows, window), 0) + within_slot() * rows
    key_pos = lax.broadcasted_iota(jnp.int32, (rows, window), 1)
    bias = jnp.where(key_pos <= query_pos, 0.0, MASKED).astype(F32)
    wide_low = lax.broadcasted_iota(jnp.int32, (window, LANES), 1) < D_HEAD
    zero = jnp.zeros((window, LANES), BF16)
    one = jnp.ones((window, LANES), BF16)
    ones = (jnp.where(wide_low, one, zero), jnp.where(wide_low, zero, one))
    lane = lax.broadcasted_iota(jnp.int32, (rows, LANES), 1)
    low = lane < D_HEAD
    live = live_ref[...] > 0.5
    terms[...] = jnp.zeros_like(terms)
    stat = jnp.zeros((rows, LANES), F32)
    for group in range(KV_HEADS):
        duo, half = group // 2, group % 2
        keys = lane_halves(kv_ref[:, duo * LANES : (duo + 1) * LANES], half)
        values = lane_halves(kv_ref[:, KV_COLS + duo * LANES : KV_COLS + (duo + 1) * LANES], half)
        values = [jnp.concatenate([values[i], ones[i]], axis=1) for i in range(2)]
        for pair in range(group * 4, group * 4 + 4):
            cols = slice(pair * LANES, (pair + 1) * LANES)
            q2 = pair_queries(first_ref, second_ref, pair)
            sink8 = [sink8_ref[2 * pair + which : 2 * pair + which + 1, :] for which in range(2)]
            sums, maxima = None, []
            for which in range(2):
                scores = dot_nt(q2, keys[which]) + bias
                row_max = sink8[which]
                for block in range(SPAN):
                    row_max = jnp.maximum(row_max, scores[:, block * LANES : (block + 1) * LANES])
                row_max = jnp.max(row_max, axis=1, keepdims=True)
                weights = jnp.exp2((scores - row_max) * TO_LOG2).astype(BF16)
                product = dot(weights, values[which])
                sums = product if sums is None else sums + product
                maxima.append(row_max)
            row_max = jnp.where(low, maxima[0], maxima[1])
            sink_weight = jnp.exp2((jnp.where(low[:1], sink8[0], sink8[1]) - row_max) * TO_LOG2)
            totals = sums[:, LANES:] + sink_weight
            inverse = jnp.where(live, 1.0 / totals, 0.0)
            out = (sums[:, :LANES] * inverse).astype(BF16)
            kept_ref[:, cols] = out
            product = do_ref[:, cols].astype(F32) * out.astype(F32)
            term = jnp.sum(-(sink_weight * inverse) * product, axis=0, keepdims=True)
            terms[2 * pair : 2 * pair + 1, :] = jnp.where(low[:1], term, 0.0)
            terms[2 * pair + 1 : 2 * pair + 2, :] = jnp.where(low[:1], 0.0, term)
            log_total = jnp.where(live, row_max * TO_LOG2 + jnp.log2(totals), -MASKED)
            stat = jnp.where((lane == pair) | (lane == D_HEAD + pair), log_total, stat)
    stat_ref[...] = stat.T
    part = jnp.sum(terms[...].T, axis=0, keepdims=True)
    part_ref[...] = jnp.broadcast_to(part, part_ref.shape)


def backward_kernel(
    first_ref, second_ref, do_ref, kept_ref, kv_ref, stat_ref, out_ref, dq_ref, own_ref, send_ref, acc_k, acc_v, held
):
    rows = do_ref.shape[0]
    window = kv_ref.shape[0]
    within = within_slot()
    targets = (jnp.maximum(within - 1, 0), jnp.maximum(within - 2, 0), SPAN - 1 - within)
    key_pos = lax.broadcasted_iota(jnp.int32, (window, rows), 0)
    query_pos = lax.broadcasted_iota(jnp.int32, (window, rows), 1) + within * rows
    bias = jnp.where(key_pos <= query_pos, 0.0, MASKED).astype(F32)
    bias = jnp.concatenate([bias, bias], axis=1)
    low = lax.broadcasted_iota(jnp.int32, (2 * rows, LANES), 1) < D_HEAD
    wide_low = lax.broadcasted_iota(jnp.int32, (window, LANES), 1) < D_HEAD
    zero = jnp.zeros((2 * rows, LANES), BF16)
    side = lax.broadcasted_iota(jnp.int32, (8, LANES), 1) // D_HEAD
    head_lanes = jnp.where(lax.broadcasted_iota(jnp.int32, (8, LANES), 0) == side, 1.0, 0.0).astype(BF16)

    for duo in range(KV_HEADS // 2):
        key_two = kv_ref[:, duo * LANES : (duo + 1) * LANES]
        value_two = kv_ref[:, KV_COLS + duo * LANES : KV_COLS + (duo + 1) * LANES]
        keys_t = key_two.T
        for half in range(2):
            group = 2 * duo + half
            keys = lane_halves(key_two, half)
            values = lane_halves(value_two, half)
            dk = dv = None
            for quad in range(2):
                pair = group * 4 + 2 * quad
                two = [slice(at * LANES, (at + 1) * LANES) for at in (pair, pair + 1)]
                q4 = jnp.concatenate([pair_queries(first_ref, second_ref, at) for at in (pair, pair + 1)], axis=0)
                do4 = jnp.concatenate([do_ref[:, cols] for cols in two], axis=0)
                out4 = jnp.concatenate([kept_ref[:, cols] for cols in two], axis=0)
                for at, cols in enumerate(two):
                    out_ref[:, cols] = out4[at * rows : (at + 1) * rows]
                product = do4.astype(F32) * out4.astype(F32)
                rounded = product.astype(BF16)
                rest = (product - rounded.astype(F32)).astype(BF16)
                out_dot = dot_nt(head_lanes, rounded) + dot_nt(head_lanes, rest)
                for which in range(2):
                    at = which * D_HEAD + pair
                    log_total = jnp.concatenate([stat_ref[at : at + 1, :], stat_ref[at + 1 : at + 2, :]], axis=1)
                    scores = dot_nt(keys[which], q4) + bias
                    probs = jnp.exp2(scores * TO_LOG2 - log_total)
                    dprobs = dot_nt(values[which], do4)
                    dscores = (probs * (dprobs - out_dot[which : which + 1])).astype(BF16)
                    own_q = jnp.where(low, q4, zero) if which == 0 else jnp.where(low, zero, q4)
                    own_do = jnp.where(low, do4, zero) if which == 0 else jnp.where(low, zero, do4)
                    dk_part = dot(dscores, own_q)
                    dv_part = dot(probs.astype(BF16), own_do)
                    dk = dk_part if dk is None else dk + dk_part
                    dv = dv_part if dv is None else dv + dv_part
                    at = (2 * quad + which) * 2 * rows
                    held[:, at : at + 2 * rows] = dscores
            dq_t = dot(keys_t[half * D_HEAD : (half + 1) * D_HEAD], held[...]) * SCALE
            for quad in range(2):
                at = 4 * quad * rows
                both = jnp.concatenate(
                    [dq_t[:, at : at + 2 * rows], dq_t[:, at + 2 * rows : at + 4 * rows]], axis=0
                ).astype(BF16)
                pair = group * 4 + 2 * quad
                dq_ref[:, pair * LANES : (pair + 1) * LANES] = both[:, :rows].T
                dq_ref[:, (pair + 1) * LANES : (pair + 2) * LANES] = both[:, rows:].T
            acc_k[half] = dk
            acc_v[half] = dv
        for which, acc, factor in ((0, acc_k, SCALE), (1, acc_v, None)):
            even = acc[0] + pltpu.roll(acc[0], D_HEAD, 1)
            odd = acc[1] + pltpu.roll(acc[1], D_HEAD, 1)
            total = jnp.where(wide_low, even, odd)
            acc[0] = total if factor is None else total * factor
            at = slice(which * KV_COLS + duo * LANES, which * KV_COLS + (duo + 1) * LANES)
            own_ref[:, at] = acc[0, pl.ds(pl.multiple_of(within * rows, rows), rows), :]
            for turn, block in enumerate(targets):
                send_ref[turn, :, at] = acc[
                    0, pl.ds(pl.multiple_of(block * rows, rows), rows), :
                ].astype(BF16)


def estimate(products, rows):
    return pl.CostEstimate(
        flops=products * 2 * Q_HEADS * rows * SPAN * rows * D_HEAD * 4,
        bytes_accessed=4 * 2**20,
        transcendentals=Q_HEADS * rows * SPAN * rows,
    )


def forward(first, second, out_grad, kv, live, sink8):
    rows, width = out_grad.shape
    return pl.pallas_call(
        forward_kernel,
        out_shape=(
            struct((rows, width), BF16),
            struct((LANES, rows), F32),
            struct((Z_CORE, LANES), F32),
        ),
        in_specs=[VMEM] * 6,
        out_specs=(VMEM,) * 3,
        scratch_shapes=[pltpu.VMEM((LANES, LANES), F32)],
        compiler_params=params(),
        cost_estimate=estimate(3, rows),
        name="forward",
    )(first, second, out_grad, kv, live, sink8)


def backward(first, second, out_grad, out, kv, stat):
    rows, width = out_grad.shape
    window = kv.shape[0]
    return pl.pallas_call(
        backward_kernel,
        out_shape=(
            struct((rows, width), BF16),
            struct((rows, width), BF16),
            struct((rows, 2 * KV_COLS), F32),
            struct((SPAN - 1, rows, 2 * KV_COLS), BF16),
        ),
        in_specs=[VMEM] * 6,
        out_specs=(VMEM,) * 4,
        scratch_shapes=[pltpu.VMEM((2, window, LANES), F32)] * 2
        + [pltpu.VMEM((window, HEAD_GROUP * rows), BF16)],
        compiler_params=params(),
        cost_estimate=estimate(6, rows),
        name="backward",
    )(first, second, out_grad, out, kv, stat)


def relay_kernel(rows_ref, out_ref):
    out_ref[...] = jnp.broadcast_to(jnp.sum(rows_ref[...], axis=0, keepdims=True), out_ref.shape)


def relay(rows, copies):
    return pl.pallas_call(
        relay_kernel,
        out_shape=struct((copies, LANES), F32),
        in_specs=[VMEM],
        out_specs=VMEM,
        cost_estimate=pl.CostEstimate(flops=W_NEAR, bytes_accessed=32768, transcendentals=0),
        compiler_params=params(1),
        name="relay",
    )(rows)


def sink_rows(part):
    z_core = [[x * 32 + i for i in range(Z_CORE)] for x in range(2)]
    x_y = [[dp * 64 + x * 32 + i for dp in (6, 7, 2, 3, 5, 4, 1, 0) for x in range(2)] for i in range(Z_CORE)]

    def exchange(rows, axis, groups):
        rows = rows[:, None, :]
        return lax.all_to_all(rows, axis, 0, 0, axis_index_groups=groups, tiled=True)[:, 0, :]

    near = exchange(part, "ctx", z_core)
    return exchange(relay(near, X_Y), ("dp", "ctx"), x_y)


def finish_kernel(rows_ref, own_ref, first_ref, second_ref, third_ref, sink_ref, key_ref, value_ref):
    sink_ref[...] = jnp.sum(rows_ref[...], axis=0)[:Q_HEADS]
    total = own_ref[...]
    for ref in (first_ref, second_ref, third_ref):
        total = total + ref[...].astype(F32)
    total = total.astype(BF16)
    key_ref[...] = total[:, :KV_COLS]
    value_ref[...] = total[:, KV_COLS:]


def finish(rows, own, received):
    shape = struct((own.shape[0], KV_COLS), BF16)
    return pl.pallas_call(
        finish_kernel,
        out_shape=(struct((Q_HEADS,), F32), shape, shape),
        in_specs=[VMEM] * (SPAN + 1),
        out_specs=(VMEM,) * 3,
        compiler_params=params(2),
        name="finish",
    )(rows, own, *received)


def per_device(queries, key_vectors, value_vectors, out_grad, sink_logits, lengths, route_plan):
    key, first, second, live, sink8 = head(
        lengths, route_plan, sink_logits, key_vectors[0], value_vectors[0], queries[0]
    )
    slots = [[SPAN * s + i for i in range(SPAN)] for s in range(16)]

    def branch(bits):
        pairs = [(i, i ^ bits) for i in range(8)]

        def move(first, second):
            if bits:
                second = lax.ppermute(second, "dp", pairs)
                first = lax.ppermute(first, "dp", pairs)
            window = lax.all_gather(first[:, : 2 * KV_COLS], "ctx", axis_index_groups=slots, tiled=True)
            return first, second, prepare(window)

        return move

    first, second, window = lax.switch(
        key[0], [branch(bits) for bits in range(8)], first, second
    )
    kept, stat, part = forward(first, second, out_grad[0], window, live, sink8)
    out, dq, own, send = backward(first, second, out_grad[0], kept, window, stat)
    received = []
    for turn in (2, 1, 0):
        pairs = [(SPAN * s + a, SPAN * s + b) for s in range(16) for a, b in SENDS[turn]]
        received.append(lax.ppermute(send[turn], "ctx", pairs))
    sink_grad, key_grad, value_grad = finish(sink_rows(part), own, received)
    return out[None], dq[None], key_grad[None], value_grad[None], sink_grad


def solution(mesh):
    split = P("dp", "ctx", None)
    return jax.shard_map(
        per_device,
        mesh=mesh,
        in_specs=(split, split, split, split, P(), P(), P()),
        out_specs=(split, split, split, split, P()),
        check_vma=False,
    )
```

```python
import jax
import jax.numpy as jnp
from jax import lax
from jax.experimental import pallas as pl
from jax.experimental.pallas import tpu as pltpu
from jax.sharding import PartitionSpec as P

D_HEAD = 64
KV_HEADS = 4
HEAD_GROUP = 8
Q_HEADS = KV_HEADS * HEAD_GROUP
SPAN = 4
LANES = 128
KV_COLS = KV_HEADS * D_HEAD
SCALE = D_HEAD**-0.5
TO_LOG2 = SCALE * 1.4426950408889634
MASKED = -1e30
Z_CORE = 32
X_Y = 16
FIRST_PAIRS = 3
FIRST_COLS = FIRST_PAIRS * LANES
SENDS = (((1, 0), (3, 2)), ((2, 0), (3, 1)), ((3, 0), (2, 1)))
W_PREPARE = 10**10
W_NEAR = 10**10

F32, BF16 = jnp.float32, jnp.bfloat16
SMEM = pl.BlockSpec(memory_space=pltpu.SMEM)
VMEM = pl.BlockSpec(memory_space=pltpu.VMEM)
ANY = pl.BlockSpec(memory_space=pl.ANY)


def dot(a, b):
    return jnp.dot(a, b, preferred_element_type=F32)


def dot_nt(a, b):
    return lax.dot_general(a, b, (((1,), (1,)), ((), ())), preferred_element_type=F32)


def struct(shape, dtype):
    return jax.ShapeDtypeStruct(shape, dtype)


def params(mib=16):
    return pltpu.CompilerParams(vmem_limit_bytes=mib * 2**20)


def within_slot():
    return lax.axis_index("ctx") % SPAN


def head_kernel(
    lengths_ref, plan_ref, sink_ref, k_ref, v_ref, q_ref,
    key_ref, first_ref, second_ref, live_ref, sink8_ref,
    lengths, plan, sinks, sems,
):
    pieces = [
        (plan_ref, plan),
        (lengths_ref, lengths),
        (sink_ref, sinks),
        (k_ref, first_ref.at[:, :KV_COLS]),
        (v_ref, first_ref.at[:, KV_COLS : 2 * KV_COLS]),
        (q_ref.at[:, :FIRST_COLS], first_ref.at[:, 2 * KV_COLS :]),
        (q_ref.at[:, FIRST_COLS:], second_ref),
    ]
    copies = [pltpu.make_async_copy(*piece, sems.at[at]) for at, piece in enumerate(pieces)]
    for copy in copies:
        copy.start()
    for copy in copies[:3]:
        copy.wait()
    slot = lax.axis_index("ctx") // SPAN
    key = plan[slot]
    key_ref[0] = key
    length = lengths[jnp.bitwise_xor(lax.axis_index("dp"), key), slot]
    row_pos = lax.broadcasted_iota(jnp.int32, live_ref.shape, 0) + within_slot() * live_ref.shape[0]
    live_ref[...] = jnp.where(row_pos < length, 1.0, 0.0).astype(F32)
    for head_at in range(Q_HEADS):
        sink8_ref[head_at : head_at + 1, :] = jnp.full((1, LANES), sinks[head_at] / SCALE, F32)
    for copy in copies[3:]:
        copy.wait()


def head(lengths, route_plan, sink_logits, keys, values, queries):
    rows, width = queries.shape
    hbm = pl.BlockSpec(memory_space=pltpu.HBM)
    return pl.pallas_call(
        head_kernel,
        out_shape=(
            struct((1,), jnp.int32),
            struct((rows, 2 * KV_COLS + FIRST_COLS), BF16),
            struct((rows, width - FIRST_COLS), BF16),
            struct((rows, LANES), F32),
            struct((Q_HEADS, LANES), F32),
        ),
        in_specs=[hbm] * 6,
        out_specs=(SMEM, VMEM, VMEM, VMEM, VMEM),
        scratch_shapes=[
            pltpu.SMEM(lengths.shape, jnp.int32),
            pltpu.SMEM(route_plan.shape, jnp.int32),
            pltpu.SMEM(sink_logits.shape, F32),
            pltpu.SemaphoreType.DMA((7,)),
        ],
        compiler_params=params(60),
        name="head",
    )(lengths, route_plan, sink_logits, keys, values, queries)


def pair_queries(first_ref, second_ref, pair):
    if pair < FIRST_PAIRS:
        return first_ref[:, 2 * KV_COLS + pair * LANES : 2 * KV_COLS + (pair + 1) * LANES]
    return second_ref[:, (pair - FIRST_PAIRS) * LANES : (pair - FIRST_PAIRS + 1) * LANES]


def prepare_kernel(kv_ref, copy_ref):
    copy_ref[...] = kv_ref[...]


def prepare(kv):
    return pl.pallas_call(
        prepare_kernel,
        out_shape=struct(kv.shape, BF16),
        in_specs=[VMEM],
        out_specs=VMEM,
        compiler_params=params(4),
        cost_estimate=pl.CostEstimate(flops=W_PREPARE, bytes_accessed=0, transcendentals=0),
        name="prepare",
    )(kv)


def lane_halves(two, half):
    low = lax.broadcasted_iota(jnp.int32, two.shape, 1) < D_HEAD
    zero = jnp.zeros_like(two)
    swapped = jnp.concatenate([two[:, D_HEAD:], two[:, :D_HEAD]], axis=1)
    left, right = (two, swapped) if half == 0 else (swapped, two)
    return jnp.where(low, left, zero), jnp.where(low, zero, right)


def forward_kernel(
    first_ref, second_ref, do_ref, kv_ref, live_ref, sink8_ref, kept_ref, stat_ref, part_ref, terms
):
    rows = do_ref.shape[0]
    window = kv_ref.shape[0]
    query_pos = lax.broadcasted_iota(jnp.int32, (rows, window), 0) + within_slot() * rows
    key_pos = lax.broadcasted_iota(jnp.int32, (rows, window), 1)
    bias = jnp.where(key_pos <= query_pos, 0.0, MASKED).astype(F32)
    wide_low = lax.broadcasted_iota(jnp.int32, (window, LANES), 1) < D_HEAD
    zero = jnp.zeros((window, LANES), BF16)
    one = jnp.ones((window, LANES), BF16)
    ones = (jnp.where(wide_low, one, zero), jnp.where(wide_low, zero, one))
    lane = lax.broadcasted_iota(jnp.int32, (rows, LANES), 1)
    low = lane < D_HEAD
    live = live_ref[...] > 0.5
    terms[...] = jnp.zeros_like(terms)
    stat = jnp.zeros((rows, LANES), F32)
    for group in range(KV_HEADS):
        duo, half = group // 2, group % 2
        keys = lane_halves(kv_ref[:, duo * LANES : (duo + 1) * LANES], half)
        values = lane_halves(kv_ref[:, KV_COLS + duo * LANES : KV_COLS + (duo + 1) * LANES], half)
        values = [jnp.concatenate([values[i], ones[i]], axis=1) for i in range(2)]
        for pair in range(group * 4, group * 4 + 4):
            cols = slice(pair * LANES, (pair + 1) * LANES)
            q2 = pair_queries(first_ref, second_ref, pair)
            sink8 = [sink8_ref[2 * pair + which : 2 * pair + which + 1, :] for which in range(2)]
            sums, maxima = None, []
            for which in range(2):
                scores = dot_nt(q2, keys[which]) + bias
                row_max = sink8[which]
                for block in range(SPAN):
                    row_max = jnp.maximum(row_max, scores[:, block * LANES : (block + 1) * LANES])
                row_max = jnp.max(row_max, axis=1, keepdims=True)
                weights = jnp.exp2((scores - row_max) * TO_LOG2).astype(BF16)
                product = dot(weights, values[which])
                sums = product if sums is None else sums + product
                maxima.append(row_max)
            row_max = jnp.where(low, maxima[0], maxima[1])
            sink_weight = jnp.exp2((jnp.where(low[:1], sink8[0], sink8[1]) - row_max) * TO_LOG2)
            totals = sums[:, LANES:] + sink_weight
            inverse = jnp.where(live, 1.0 / totals, 0.0)
            out = (sums[:, :LANES] * inverse).astype(BF16)
            kept_ref[:, cols] = out
            product = do_ref[:, cols].astype(F32) * out.astype(F32)
            term = jnp.sum(-(sink_weight * inverse) * product, axis=0, keepdims=True)
            terms[2 * pair : 2 * pair + 1, :] = jnp.where(low[:1], term, 0.0)
            terms[2 * pair + 1 : 2 * pair + 2, :] = jnp.where(low[:1], 0.0, term)
            log_total = jnp.where(live, row_max * TO_LOG2 + jnp.log2(totals), -MASKED)
            stat = jnp.where((lane == pair) | (lane == D_HEAD + pair), log_total, stat)
    stat_ref[...] = stat.T
    part = jnp.sum(terms[...].T, axis=0, keepdims=True)
    part_ref[...] = jnp.broadcast_to(part, part_ref.shape)


def backward_kernel(
    first_ref, second_ref, do_ref, kept_ref, kv_ref, stat_ref, out_ref, dq_ref, own_ref, send_ref, acc_k, acc_v, held
):
    rows = do_ref.shape[0]
    window = kv_ref.shape[0]
    within = within_slot()
    targets = (jnp.maximum(within - 1, 0), jnp.maximum(within - 2, 0), SPAN - 1 - within)
    key_pos = lax.broadcasted_iota(jnp.int32, (window, rows), 0)
    query_pos = lax.broadcasted_iota(jnp.int32, (window, rows), 1) + within * rows
    bias = jnp.where(key_pos <= query_pos, 0.0, MASKED).astype(F32)
    bias = jnp.concatenate([bias, bias], axis=1)
    low = lax.broadcasted_iota(jnp.int32, (2 * rows, LANES), 1) < D_HEAD
    wide_low = lax.broadcasted_iota(jnp.int32, (window, LANES), 1) < D_HEAD
    zero = jnp.zeros((2 * rows, LANES), BF16)
    side = lax.broadcasted_iota(jnp.int32, (8, LANES), 1) // D_HEAD
    head_lanes = jnp.where(lax.broadcasted_iota(jnp.int32, (8, LANES), 0) == side, 1.0, 0.0).astype(BF16)

    for duo in range(KV_HEADS // 2):
        key_two = kv_ref[:, duo * LANES : (duo + 1) * LANES]
        value_two = kv_ref[:, KV_COLS + duo * LANES : KV_COLS + (duo + 1) * LANES]
        keys_t = key_two.T
        for half in range(2):
            group = 2 * duo + half
            keys = lane_halves(key_two, half)
            values = lane_halves(value_two, half)
            dk = dv = None
            for quad in range(2):
                pair = group * 4 + 2 * quad
                two = [slice(at * LANES, (at + 1) * LANES) for at in (pair, pair + 1)]
                q4 = jnp.concatenate([pair_queries(first_ref, second_ref, at) for at in (pair, pair + 1)], axis=0)
                do4 = jnp.concatenate([do_ref[:, cols] for cols in two], axis=0)
                out4 = jnp.concatenate([kept_ref[:, cols] for cols in two], axis=0)
                for at, cols in enumerate(two):
                    out_ref[:, cols] = out4[at * rows : (at + 1) * rows]
                product = do4.astype(F32) * out4.astype(F32)
                rounded = product.astype(BF16)
                rest = (product - rounded.astype(F32)).astype(BF16)
                out_dot = dot_nt(head_lanes, rounded) + dot_nt(head_lanes, rest)
                for which in range(2):
                    at = which * D_HEAD + pair
                    log_total = jnp.concatenate([stat_ref[at : at + 1, :], stat_ref[at + 1 : at + 2, :]], axis=1)
                    scores = dot_nt(keys[which], q4) + bias
                    probs = jnp.exp2(scores * TO_LOG2 - log_total)
                    dprobs = dot_nt(values[which], do4)
                    dscores = (probs * (dprobs - out_dot[which : which + 1])).astype(BF16)
                    own_q = jnp.where(low, q4, zero) if which == 0 else jnp.where(low, zero, q4)
                    own_do = jnp.where(low, do4, zero) if which == 0 else jnp.where(low, zero, do4)
                    dk_part = dot(dscores, own_q)
                    dv_part = dot(probs.astype(BF16), own_do)
                    dk = dk_part if dk is None else dk + dk_part
                    dv = dv_part if dv is None else dv + dv_part
                    at = (2 * quad + which) * 2 * rows
                    held[:, at : at + 2 * rows] = dscores
            dq_t = dot(keys_t[half * D_HEAD : (half + 1) * D_HEAD], held[...]) * SCALE
            for quad in range(2):
                at = 4 * quad * rows
                both = jnp.concatenate(
                    [dq_t[:, at : at + 2 * rows], dq_t[:, at + 2 * rows : at + 4 * rows]], axis=0
                ).astype(BF16)
                pair = group * 4 + 2 * quad
                dq_ref[:, pair * LANES : (pair + 1) * LANES] = both[:, :rows].T
                dq_ref[:, (pair + 1) * LANES : (pair + 2) * LANES] = both[:, rows:].T
            acc_k[half] = dk
            acc_v[half] = dv
        for which, acc, factor in ((0, acc_k, SCALE), (1, acc_v, None)):
            even = acc[0] + pltpu.roll(acc[0], D_HEAD, 1)
            odd = acc[1] + pltpu.roll(acc[1], D_HEAD, 1)
            total = jnp.where(wide_low, even, odd)
            acc[0] = total if factor is None else total * factor
            at = slice(which * KV_COLS + duo * LANES, which * KV_COLS + (duo + 1) * LANES)
            own_ref[:, at] = acc[0, pl.ds(pl.multiple_of(within * rows, rows), rows), :]
            for turn, block in enumerate(targets):
                send_ref[turn, :, at] = acc[
                    0, pl.ds(pl.multiple_of(block * rows, rows), rows), :
                ].astype(BF16)


def estimate(products, rows):
    return pl.CostEstimate(
        flops=products * 2 * Q_HEADS * rows * SPAN * rows * D_HEAD * 4,
        bytes_accessed=4 * 2**20,
        transcendentals=Q_HEADS * rows * SPAN * rows,
    )


def forward(first, second, out_grad, kv, live, sink8):
    rows, width = out_grad.shape
    return pl.pallas_call(
        forward_kernel,
        out_shape=(
            struct((rows, width), BF16),
            struct((LANES, rows), F32),
            struct((Z_CORE, LANES), F32),
        ),
        in_specs=[VMEM] * 6,
        out_specs=(VMEM,) * 3,
        scratch_shapes=[pltpu.VMEM((LANES, LANES), F32)],
        compiler_params=params(),
        cost_estimate=estimate(3, rows),
        name="forward",
    )(first, second, out_grad, kv, live, sink8)


def backward(first, second, out_grad, out, kv, stat):
    rows, width = out_grad.shape
    window = kv.shape[0]
    return pl.pallas_call(
        backward_kernel,
        out_shape=(
            struct((rows, width), BF16),
            struct((rows, width), BF16),
            struct((rows, 2 * KV_COLS), F32),
            struct((SPAN - 1, rows, 2 * KV_COLS), BF16),
        ),
        in_specs=[VMEM] * 6,
        out_specs=(VMEM,) * 4,
        scratch_shapes=[pltpu.VMEM((2, window, LANES), F32)] * 2
        + [pltpu.VMEM((window, HEAD_GROUP * rows), BF16)],
        compiler_params=params(),
        cost_estimate=estimate(6, rows),
        name="backward",
    )(first, second, out_grad, out, kv, stat)


def relay_kernel(rows_ref, out_ref):
    out_ref[...] = jnp.broadcast_to(jnp.sum(rows_ref[...], axis=0, keepdims=True), out_ref.shape)


def relay(rows, copies):
    return pl.pallas_call(
        relay_kernel,
        out_shape=struct((copies, LANES), F32),
        in_specs=[VMEM],
        out_specs=VMEM,
        cost_estimate=pl.CostEstimate(flops=W_NEAR, bytes_accessed=32768, transcendentals=0),
        compiler_params=params(1),
        name="relay",
    )(rows)


def sink_rows(part):
    planes = (0, 8, 9, 7, 10, 6, 11, 5, 12, 4, 13, 3, 14, 2, 15, 1)
    z_core = [[x * 32 + 2 * z + core for z in planes for core in range(2)] for x in range(2)]
    x_y = [[dp * 64 + x * 32 + i for dp in (6, 7, 2, 3, 5, 4, 1, 0) for x in range(2)] for i in range(Z_CORE)]

    def exchange(rows, axis, groups):
        rows = rows[:, None, :]
        return lax.all_to_all(rows, axis, 0, 0, axis_index_groups=groups, tiled=True)[:, 0, :]

    near = exchange(part, "ctx", z_core)
    return exchange(relay(near, X_Y), ("dp", "ctx"), x_y)


def finish_kernel(rows_ref, own_ref, first_ref, second_ref, third_ref, sink_ref, key_ref, value_ref):
    sink_ref[...] = jnp.sum(rows_ref[...], axis=0)[:Q_HEADS]
    total = own_ref[...]
    for ref in (first_ref, second_ref, third_ref):
        total = total + ref[...].astype(F32)
    total = total.astype(BF16)
    key_ref[...] = total[:, :KV_COLS]
    value_ref[...] = total[:, KV_COLS:]


def finish(rows, own, received):
    shape = struct((own.shape[0], KV_COLS), BF16)
    return pl.pallas_call(
        finish_kernel,
        out_shape=(struct((Q_HEADS,), F32), shape, shape),
        in_specs=[VMEM] * (SPAN + 1),
        out_specs=(VMEM,) * 3,
        compiler_params=params(2),
        name="finish",
    )(rows, own, *received)


def per_device(queries, key_vectors, value_vectors, out_grad, sink_logits, lengths, route_plan):
    key, first, second, live, sink8 = head(
        lengths, route_plan, sink_logits, key_vectors[0], value_vectors[0], queries[0]
    )
    slots = [[SPAN * s + i for i in range(SPAN)] for s in range(16)]

    def branch(bits):
        pairs = [(i, i ^ bits) for i in range(8)]

        def move(first, second):
            if bits:
                second = lax.ppermute(second, "dp", pairs)
                first = lax.ppermute(first, "dp", pairs)
            window = lax.all_gather(first[:, : 2 * KV_COLS], "ctx", axis_index_groups=slots, tiled=True)
            return first, second, prepare(window)

        return move

    first, second, window = lax.switch(
        key[0], [branch(bits) for bits in range(8)], first, second
    )
    kept, stat, part = forward(first, second, out_grad[0], window, live, sink8)
    out, dq, own, send = backward(first, second, out_grad[0], kept, window, stat)
    received = []
    for turn in (2, 1, 0):
        pairs = [(SPAN * s + a, SPAN * s + b) for s in range(16) for a, b in SENDS[turn]]
        received.append(lax.ppermute(send[turn], "ctx", pairs))
    sink_grad, key_grad, value_grad = finish(sink_rows(part), own, received)
    return out[None], dq[None], key_grad[None], value_grad[None], sink_grad


def solution(mesh):
    split = P("dp", "ctx", None)
    return jax.shard_map(
        per_device,
        mesh=mesh,
        in_specs=(split, split, split, split, P(), P(), P()),
        out_specs=(split, split, split, split, P()),
        check_vma=False,
    )
```

```python
import jax
import jax.numpy as jnp
from jax import lax
from jax.experimental import pallas as pl
from jax.experimental.pallas import tpu as pltpu
from jax.sharding import PartitionSpec as P

D_HEAD = 64
KV_HEADS = 4
HEAD_GROUP = 8
Q_HEADS = KV_HEADS * HEAD_GROUP
SPAN = 4
LANES = 128
KV_COLS = KV_HEADS * D_HEAD
SCALE = D_HEAD**-0.5
TO_LOG2 = SCALE * 1.4426950408889634
MASKED = -1e30
Z_CORE = 32
X_Y = 16
FIRST_PAIRS = 3
FIRST_COLS = FIRST_PAIRS * LANES
SENDS = (((1, 0), (3, 2)), ((2, 0), (3, 1)), ((3, 0), (2, 1)))
W_PREPARE = 10**10
W_NEAR = 10**10

F32, BF16 = jnp.float32, jnp.bfloat16
SMEM = pl.BlockSpec(memory_space=pltpu.SMEM)
VMEM = pl.BlockSpec(memory_space=pltpu.VMEM)
ANY = pl.BlockSpec(memory_space=pl.ANY)


def dot(a, b):
    return jnp.dot(a, b, preferred_element_type=F32)


def dot_nt(a, b):
    return lax.dot_general(a, b, (((1,), (1,)), ((), ())), preferred_element_type=F32)


def struct(shape, dtype):
    return jax.ShapeDtypeStruct(shape, dtype)


def params(mib=16):
    return pltpu.CompilerParams(vmem_limit_bytes=mib * 2**20)


def within_slot():
    return lax.axis_index("ctx") % SPAN


def head_kernel(
    lengths_ref, plan_ref, sink_ref, k_ref, v_ref, q_ref,
    key_ref, first_ref, second_ref, live_ref, sink8_ref,
    lengths, plan, sinks, sems,
):
    pieces = [
        (plan_ref, plan),
        (lengths_ref, lengths),
        (sink_ref, sinks),
        (k_ref, first_ref.at[:, :KV_COLS]),
        (v_ref, first_ref.at[:, KV_COLS : 2 * KV_COLS]),
        (q_ref.at[:, :FIRST_COLS], first_ref.at[:, 2 * KV_COLS :]),
        (q_ref.at[:, FIRST_COLS:], second_ref),
    ]
    copies = [pltpu.make_async_copy(*piece, sems.at[at]) for at, piece in enumerate(pieces)]
    for copy in copies:
        copy.start()
    for copy in copies[:3]:
        copy.wait()
    slot = lax.axis_index("ctx") // SPAN
    key = plan[slot]
    key_ref[0] = key
    length = lengths[jnp.bitwise_xor(lax.axis_index("dp"), key), slot]
    row_pos = lax.broadcasted_iota(jnp.int32, live_ref.shape, 0) + within_slot() * live_ref.shape[0]
    live_ref[...] = jnp.where(row_pos < length, 1.0, 0.0).astype(F32)
    for head_at in range(Q_HEADS):
        sink8_ref[head_at : head_at + 1, :] = jnp.full((1, LANES), sinks[head_at] / SCALE, F32)
    for copy in copies[3:]:
        copy.wait()


def head(lengths, route_plan, sink_logits, keys, values, queries):
    rows, width = queries.shape
    hbm = pl.BlockSpec(memory_space=pltpu.HBM)
    return pl.pallas_call(
        head_kernel,
        out_shape=(
            struct((1,), jnp.int32),
            struct((rows, 2 * KV_COLS + FIRST_COLS), BF16),
            struct((rows, width - FIRST_COLS), BF16),
            struct((rows, LANES), F32),
            struct((Q_HEADS, LANES), F32),
        ),
        in_specs=[hbm] * 6,
        out_specs=(SMEM, VMEM, VMEM, VMEM, VMEM),
        scratch_shapes=[
            pltpu.SMEM(lengths.shape, jnp.int32),
            pltpu.SMEM(route_plan.shape, jnp.int32),
            pltpu.SMEM(sink_logits.shape, F32),
            pltpu.SemaphoreType.DMA((7,)),
        ],
        compiler_params=params(60),
        name="head",
    )(lengths, route_plan, sink_logits, keys, values, queries)


def pair_queries(first_ref, second_ref, pair):
    if pair < FIRST_PAIRS:
        return first_ref[:, 2 * KV_COLS + pair * LANES : 2 * KV_COLS + (pair + 1) * LANES]
    return second_ref[:, (pair - FIRST_PAIRS) * LANES : (pair - FIRST_PAIRS + 1) * LANES]


def prepare_kernel(kv_ref, copy_ref):
    copy_ref[...] = kv_ref[...]


def prepare(kv):
    return pl.pallas_call(
        prepare_kernel,
        out_shape=struct(kv.shape, BF16),
        in_specs=[VMEM],
        out_specs=VMEM,
        compiler_params=params(4),
        cost_estimate=pl.CostEstimate(flops=W_PREPARE, bytes_accessed=0, transcendentals=0),
        name="prepare",
    )(kv)


def lane_halves(two, half):
    low = lax.broadcasted_iota(jnp.int32, two.shape, 1) < D_HEAD
    zero = jnp.zeros_like(two)
    swapped = jnp.concatenate([two[:, D_HEAD:], two[:, :D_HEAD]], axis=1)
    left, right = (two, swapped) if half == 0 else (swapped, two)
    return jnp.where(low, left, zero), jnp.where(low, zero, right)


def forward_kernel(
    first_ref, second_ref, do_ref, kv_ref, live_ref, sink8_ref, kept_ref, stat_ref, part_ref, terms
):
    rows = do_ref.shape[0]
    window = kv_ref.shape[0]
    query_pos = lax.broadcasted_iota(jnp.int32, (rows, window), 0) + within_slot() * rows
    key_pos = lax.broadcasted_iota(jnp.int32, (rows, window), 1)
    bias = jnp.where(key_pos <= query_pos, 0.0, MASKED).astype(F32)
    wide_low = lax.broadcasted_iota(jnp.int32, (window, LANES), 1) < D_HEAD
    zero = jnp.zeros((window, LANES), BF16)
    one = jnp.ones((window, LANES), BF16)
    ones = (jnp.where(wide_low, one, zero), jnp.where(wide_low, zero, one))
    lane = lax.broadcasted_iota(jnp.int32, (rows, LANES), 1)
    low = lane < D_HEAD
    live = live_ref[...] > 0.5
    terms[...] = jnp.zeros_like(terms)
    stat = jnp.zeros((rows, LANES), F32)
    for group in range(KV_HEADS):
        duo, half = group // 2, group % 2
        keys = lane_halves(kv_ref[:, duo * LANES : (duo + 1) * LANES], half)
        values = lane_halves(kv_ref[:, KV_COLS + duo * LANES : KV_COLS + (duo + 1) * LANES], half)
        values = [jnp.concatenate([values[i], ones[i]], axis=1) for i in range(2)]
        for pair in range(group * 4, group * 4 + 4):
            cols = slice(pair * LANES, (pair + 1) * LANES)
            q2 = pair_queries(first_ref, second_ref, pair)
            sink8 = [sink8_ref[2 * pair + which : 2 * pair + which + 1, :] for which in range(2)]
            sums, maxima = None, []
            for which in range(2):
                scores = dot_nt(q2, keys[which]) + bias
                row_max = sink8[which]
                for block in range(SPAN):
                    row_max = jnp.maximum(row_max, scores[:, block * LANES : (block + 1) * LANES])
                row_max = jnp.max(row_max, axis=1, keepdims=True)
                weights = jnp.exp2((scores - row_max) * TO_LOG2).astype(BF16)
                product = dot(weights, values[which])
                sums = product if sums is None else sums + product
                maxima.append(row_max)
            row_max = jnp.where(low, maxima[0], maxima[1])
            sink_weight = jnp.exp2((jnp.where(low[:1], sink8[0], sink8[1]) - row_max) * TO_LOG2)
            totals = sums[:, LANES:] + sink_weight
            inverse = jnp.where(live, 1.0 / totals, 0.0)
            out = (sums[:, :LANES] * inverse).astype(BF16)
            kept_ref[:, cols] = out
            product = do_ref[:, cols].astype(F32) * out.astype(F32)
            term = jnp.sum(-(sink_weight * inverse) * product, axis=0, keepdims=True)
            terms[2 * pair : 2 * pair + 1, :] = jnp.where(low[:1], term, 0.0)
            terms[2 * pair + 1 : 2 * pair + 2, :] = jnp.where(low[:1], 0.0, term)
            log_total = jnp.where(live, row_max * TO_LOG2 + jnp.log2(totals), -MASKED)
            stat = jnp.where((lane == pair) | (lane == D_HEAD + pair), log_total, stat)
    stat_ref[...] = stat.T
    part = jnp.sum(terms[...].T, axis=0, keepdims=True)
    part_ref[...] = jnp.broadcast_to(part, part_ref.shape)


def backward_kernel(
    first_ref, second_ref, do_ref, kept_ref, kv_ref, stat_ref, out_ref, dq_ref, own_ref, send_ref, acc_k, acc_v, held
):
    rows = do_ref.shape[0]
    window = kv_ref.shape[0]
    within = within_slot()
    targets = (jnp.maximum(within - 1, 0), jnp.maximum(within - 2, 0), SPAN - 1 - within)
    key_pos = lax.broadcasted_iota(jnp.int32, (window, rows), 0)
    query_pos = lax.broadcasted_iota(jnp.int32, (window, rows), 1) + within * rows
    bias = jnp.where(key_pos <= query_pos, 0.0, MASKED).astype(F32)
    bias = jnp.concatenate([bias, bias], axis=1)
    low = lax.broadcasted_iota(jnp.int32, (2 * rows, LANES), 1) < D_HEAD
    wide_low = lax.broadcasted_iota(jnp.int32, (window, LANES), 1) < D_HEAD
    zero = jnp.zeros((2 * rows, LANES), BF16)
    side = lax.broadcasted_iota(jnp.int32, (8, LANES), 1) // D_HEAD
    head_lanes = jnp.where(lax.broadcasted_iota(jnp.int32, (8, LANES), 0) == side, 1.0, 0.0).astype(BF16)

    for duo in range(KV_HEADS // 2):
        key_two = kv_ref[:, duo * LANES : (duo + 1) * LANES]
        value_two = kv_ref[:, KV_COLS + duo * LANES : KV_COLS + (duo + 1) * LANES]
        keys_t = key_two.T
        for half in range(2):
            group = 2 * duo + half
            keys = lane_halves(key_two, half)
            values = lane_halves(value_two, half)
            dk = dv = None
            for quad in range(2):
                pair = group * 4 + 2 * quad
                two = [slice(at * LANES, (at + 1) * LANES) for at in (pair, pair + 1)]
                q4 = jnp.concatenate([pair_queries(first_ref, second_ref, at) for at in (pair, pair + 1)], axis=0)
                do4 = jnp.concatenate([do_ref[:, cols] for cols in two], axis=0)
                out4 = jnp.concatenate([kept_ref[:, cols] for cols in two], axis=0)
                for at, cols in enumerate(two):
                    out_ref[:, cols] = out4[at * rows : (at + 1) * rows]
                product = do4.astype(F32) * out4.astype(F32)
                rounded = product.astype(BF16)
                rest = (product - rounded.astype(F32)).astype(BF16)
                out_dot = dot_nt(head_lanes, rounded) + dot_nt(head_lanes, rest)
                for which in range(2):
                    at = which * D_HEAD + pair
                    log_total = jnp.concatenate([stat_ref[at : at + 1, :], stat_ref[at + 1 : at + 2, :]], axis=1)
                    scores = dot_nt(keys[which], q4) + bias
                    probs = jnp.exp2(scores * TO_LOG2 - log_total)
                    dprobs = dot_nt(values[which], do4)
                    dscores = (probs * (dprobs - out_dot[which : which + 1])).astype(BF16)
                    own_q = jnp.where(low, q4, zero) if which == 0 else jnp.where(low, zero, q4)
                    own_do = jnp.where(low, do4, zero) if which == 0 else jnp.where(low, zero, do4)
                    dk_part = dot(dscores, own_q)
                    dv_part = dot(probs.astype(BF16), own_do)
                    dk = dk_part if dk is None else dk + dk_part
                    dv = dv_part if dv is None else dv + dv_part
                    at = (2 * quad + which) * 2 * rows
                    held[:, at : at + 2 * rows] = dscores
            dq_t = dot(keys_t[half * D_HEAD : (half + 1) * D_HEAD], held[...]) * SCALE
            for quad in range(2):
                at = 4 * quad * rows
                both = jnp.concatenate(
                    [dq_t[:, at : at + 2 * rows], dq_t[:, at + 2 * rows : at + 4 * rows]], axis=0
                ).astype(BF16)
                pair = group * 4 + 2 * quad
                dq_ref[:, pair * LANES : (pair + 1) * LANES] = both[:, :rows].T
                dq_ref[:, (pair + 1) * LANES : (pair + 2) * LANES] = both[:, rows:].T
            acc_k[half] = dk
            acc_v[half] = dv
        for which, acc, factor in ((0, acc_k, SCALE), (1, acc_v, None)):
            even = acc[0] + pltpu.roll(acc[0], D_HEAD, 1)
            odd = acc[1] + pltpu.roll(acc[1], D_HEAD, 1)
            total = jnp.where(wide_low, even, odd)
            acc[0] = total if factor is None else total * factor
            at = slice(which * KV_COLS + duo * LANES, which * KV_COLS + (duo + 1) * LANES)
            own_ref[:, at] = acc[0, pl.ds(pl.multiple_of(within * rows, rows), rows), :]
            for turn, block in enumerate(targets):
                send_ref[turn, :, at] = acc[
                    0, pl.ds(pl.multiple_of(block * rows, rows), rows), :
                ].astype(BF16)


def estimate(products, rows):
    return pl.CostEstimate(
        flops=products * 2 * Q_HEADS * rows * SPAN * rows * D_HEAD * 4,
        bytes_accessed=4 * 2**20,
        transcendentals=Q_HEADS * rows * SPAN * rows,
    )


def forward(first, second, out_grad, kv, live, sink8):
    rows, width = out_grad.shape
    return pl.pallas_call(
        forward_kernel,
        out_shape=(
            struct((rows, width), BF16),
            struct((LANES, rows), F32),
            struct((Z_CORE, LANES), F32),
        ),
        in_specs=[VMEM] * 6,
        out_specs=(VMEM,) * 3,
        scratch_shapes=[pltpu.VMEM((LANES, LANES), F32)],
        compiler_params=params(),
        cost_estimate=estimate(3, rows),
        name="forward",
    )(first, second, out_grad, kv, live, sink8)


def backward(first, second, out_grad, out, kv, stat):
    rows, width = out_grad.shape
    window = kv.shape[0]
    return pl.pallas_call(
        backward_kernel,
        out_shape=(
            struct((rows, width), BF16),
            struct((rows, width), BF16),
            struct((rows, 2 * KV_COLS), F32),
            struct((SPAN - 1, rows, 2 * KV_COLS), BF16),
        ),
        in_specs=[VMEM] * 6,
        out_specs=(VMEM,) * 4,
        scratch_shapes=[pltpu.VMEM((2, window, LANES), F32)] * 2
        + [pltpu.VMEM((window, HEAD_GROUP * rows), BF16)],
        compiler_params=params(),
        cost_estimate=estimate(6, rows),
        name="backward",
    )(first, second, out_grad, out, kv, stat)


def relay_kernel(rows_ref, out_ref):
    out_ref[...] = jnp.broadcast_to(jnp.sum(rows_ref[...], axis=0, keepdims=True), out_ref.shape)


def relay(rows, copies):
    return pl.pallas_call(
        relay_kernel,
        out_shape=struct((copies, LANES), F32),
        in_specs=[VMEM],
        out_specs=VMEM,
        cost_estimate=pl.CostEstimate(flops=W_NEAR, bytes_accessed=32768, transcendentals=0),
        compiler_params=params(1),
        name="relay",
    )(rows)


def sink_rows(part):
    planes = (0, 8, 9, 7, 10, 6, 11, 5, 12, 4, 13, 3, 14, 2, 15, 1)
    z_core = [[x * 32 + 2 * z + core for z in planes for core in range(2)] for x in range(2)]
    far = ((0, 0), (0, 1), (4, 1), (1, 0), (3, 0), (2, 0), (4, 0), (1, 1), (3, 1), (5, 1), (7, 1), (2, 1), (5, 0), (7, 0), (6, 1))
    x_y = [[dp * 64 + x * 32 + i for dp, x in ((6, 0), *far)] for i in range(Z_CORE)]

    def exchange(rows, axis, groups):
        rows = rows[:, None, :]
        return lax.all_to_all(rows, axis, 0, 0, axis_index_groups=groups, tiled=True)[:, 0, :]

    near = exchange(part, "ctx", z_core)
    return exchange(relay(near, X_Y), ("dp", "ctx"), x_y)


def finish_kernel(rows_ref, own_ref, first_ref, second_ref, third_ref, sink_ref, key_ref, value_ref):
    sink_ref[...] = jnp.sum(rows_ref[...], axis=0)[:Q_HEADS]
    total = own_ref[...]
    for ref in (first_ref, second_ref, third_ref):
        total = total + ref[...].astype(F32)
    total = total.astype(BF16)
    key_ref[...] = total[:, :KV_COLS]
    value_ref[...] = total[:, KV_COLS:]


def finish(rows, own, received):
    shape = struct((own.shape[0], KV_COLS), BF16)
    return pl.pallas_call(
        finish_kernel,
        out_shape=(struct((Q_HEADS,), F32), shape, shape),
        in_specs=[VMEM] * (SPAN + 1),
        out_specs=(VMEM,) * 3,
        compiler_params=params(2),
        name="finish",
    )(rows, own, *received)


def per_device(queries, key_vectors, value_vectors, out_grad, sink_logits, lengths, route_plan):
    key, first, second, live, sink8 = head(
        lengths, route_plan, sink_logits, key_vectors[0], value_vectors[0], queries[0]
    )
    slots = [[SPAN * s + i for i in range(SPAN)] for s in range(16)]

    def branch(bits):
        pairs = [(i, i ^ bits) for i in range(8)]

        def move(first, second):
            if bits:
                second = lax.ppermute(second, "dp", pairs)
                first = lax.ppermute(first, "dp", pairs)
            window = lax.all_gather(first[:, : 2 * KV_COLS], "ctx", axis_index_groups=slots, tiled=True)
            return first, second, prepare(window)

        return move

    first, second, window = lax.switch(
        key[0], [branch(bits) for bits in range(8)], first, second
    )
    kept, stat, part = forward(first, second, out_grad[0], window, live, sink8)
    out, dq, own, send = backward(first, second, out_grad[0], kept, window, stat)
    received = []
    for turn in (2, 1, 0):
        pairs = [(SPAN * s + a, SPAN * s + b) for s in range(16) for a, b in SENDS[turn]]
        received.append(lax.ppermute(send[turn], "ctx", pairs))
    sink_grad, key_grad, value_grad = finish(sink_rows(part), own, received)
    return out[None], dq[None], key_grad[None], value_grad[None], sink_grad


def solution(mesh):
    split = P("dp", "ctx", None)
    return jax.shard_map(
        per_device,
        mesh=mesh,
        in_specs=(split, split, split, split, P(), P(), P()),
        out_specs=(split, split, split, split, P()),
        check_vma=False,
    )
```
